256 devices in a mesh: src: 32 (over z, x), tgt: 8 (over y, core).
Axes of the slice: x: 4, y: 4, z: 8, core: 2. Of those that a mesh axis runs over, the one named last changes fastest.
Arguments:
- src_points: float32 [50, 524288], P(None, 'src')
- tgt_points: float32 [50, 196608], P(None, 'tgt')
- tiles: int32 [32, 8, 2, 32], P('src', 'tgt'), may hold values from 0 to 95, as said below
- counts: int32 [32, 8], P('src', 'tgt'), may hold values from 8 to 32, as said below
Outputs:
- source_potential: float32 [524288], P('src')
- target_potential: float32 [196608], P('tgt')
The draws below stay inside these ranges and needn't reach their ends.
Inputs may be any that keep to these rules, and one draw needn't show every extreme that they name: tiles[i, j, 0, k] is a row block below 64 and tiles[i, j, 1, k] a column block below 96; the pairs of the live slots of one device are distinct; each source block of src index i is in a live slot of some device (i, j), each target block of tgt index j in a live slot of some device (i, j). The live slots of device (i, j) are its first counts[i, j] slots.
All inputs are finite; a program needn't handle non-finite values.
Results may differ from the reference program's by a relative error of at most 0.0003.
Values sent between devices are 32-bit elements; how exact they have to be, the bound alone decides.
No kernel may reach another device: no remote copies, remote signals or barrier semaphores. Data moves between devices by JAX's collectives and lax.ppermute only.
A program may use at most 128 MiB of HBM per device.

```python
import jax
import jax.numpy as jnp
from jax import lax

PC = 50
TILE = 256
RB = 64
CB = 96
KT = 32
ITERS = 3
NS = 524288
NT = 196608
N_SRC = 32
N_TGT = 8


def tile_table(key):
    mand = max(RB // N_TGT, CB // N_SRC)
    spare = KT - mand
    src_index = jnp.arange(N_SRC, dtype=jnp.int32)[:, None, None]
    tgt_index = jnp.arange(N_TGT, dtype=jnp.int32)[None, :, None]
    slot = jnp.arange(mand, dtype=jnp.int32)[None, None, :]
    rows_first = tgt_index + N_TGT * (slot % (RB // N_TGT))
    cols_first = src_index + N_SRC * (slot % (CB // N_SRC))
    rows_first = jnp.broadcast_to(rows_first, (N_SRC, N_TGT, mand))
    cols_first = jnp.broadcast_to(cols_first, (N_SRC, N_TGT, mand))
    flat = jnp.arange(RB * CB, dtype=jnp.int32)[None, None, :]
    special = (flat // CB % N_TGT == tgt_index) & (flat % CB % N_SRC == src_index)
    score = jax.random.randint(jax.random.fold_in(key, 11), (N_SRC, N_TGT, RB * CB), 0, 2 ** 20)
    score = score + special.astype(jnp.int32) * 2 ** 21
    order = jnp.argsort(score, axis=2, stable=True)[:, :, :spare].astype(jnp.int32)
    rows = jnp.concatenate([rows_first, order // CB], axis=2)
    cols = jnp.concatenate([cols_first, order % CB], axis=2)
    raw = jax.random.randint(jax.random.fold_in(key, 12), (N_SRC * N_TGT,), 0, spare + 1)
    busiest = jax.random.randint(jax.random.fold_in(key, 13), (), 0, N_SRC * N_TGT)
    raw = jnp.where(jnp.arange(N_SRC * N_TGT, dtype=jnp.int32) == busiest, spare, raw)
    live = mand + raw * raw * raw // max(spare * spare, 1)
    return (jnp.stack([rows, cols], axis=2), live.reshape(N_SRC, N_TGT))


def point_cloud(key, cells, moved):
    base = jax.random.normal(key, (PC, cells), jnp.float32)
    points = base * 0.1
    if moved:
        chosen = jax.random.randint(jax.random.fold_in(key, 22), (cells,), 0, 16) == 0
        level = jax.random.randint(jax.random.fold_in(key, 23), (cells,), 0, 3).astype(jnp.float32)
        reach = jnp.where(chosen, jnp.sqrt(6.0 + 4.0 * level), 0.0)
        points = points.at[0].add(reach)
    return points


def draw_tiles(key, part):
    table, live = tile_table(key)
    return table


def draw_counts(key, part):
    table, live = tile_table(key)
    return live


def draw_src_points(key, part):
    key = jax.random.fold_in(key, 3)
    return point_cloud(key, NS, True)


def draw_tgt_points(key, part):
    key = jax.random.fold_in(key, 4)
    return point_cloud(key, NT, False)


def setup_inputs(seed: int = 0) -> dict:
    streams_of = jax.random.split(jax.random.key(seed), 5)
    src_points = draw_src_points(jax.random.fold_in(streams_of[4], 71), 0)
    tgt_points = draw_tgt_points(jax.random.fold_in(streams_of[4], 71), 0)
    tiles = draw_tiles(jax.random.fold_in(streams_of[4], 71), 0)
    counts = draw_counts(jax.random.fold_in(streams_of[4], 71), 0)
    return {"src_points": src_points, "tgt_points": tgt_points, "tiles": tiles, "counts": counts}


EPS = 0.05
FLOOR = -1.0e30


def combine(first, second):
    top = jnp.maximum(first[0], second[0])
    return top, first[1] * jnp.exp(first[0] - top) + second[1] * jnp.exp(second[0] - top)


def tile_costs(src_shard, tgt_shard, rows, cols):
    src_tiles = jnp.take(src_shard.reshape(src_shard.shape[0], -1, TILE), rows, axis=1)
    tgt_tiles = jnp.take(tgt_shard.reshape(tgt_shard.shape[0], -1, TILE), cols, axis=1)
    cross = jnp.einsum('pka,pkb->kab', src_tiles, tgt_tiles, precision=lax.Precision.HIGHEST)
    src_square = jnp.sum(src_tiles * src_tiles, axis=0)
    tgt_square = jnp.sum(tgt_tiles * tgt_tiles, axis=0)
    return src_square[:, :, None] + tgt_square[:, None, :] - 2.0 * cross


def block_partial(scores, axis_num, live, blocks, num_blocks):
    peak = jnp.max(scores, axis=axis_num)
    total = jnp.sum(jnp.exp(scores - jnp.expand_dims(peak, axis_num)), axis=axis_num)
    peak = jnp.where(live[:, None], peak, FLOOR)
    total = jnp.where(live[:, None], total, 0.0)
    select = blocks[:, None] == jnp.arange(num_blocks, dtype=jnp.int32)[None, :]
    top = jnp.max(jnp.where(select[:, :, None], peak[:, None, :], FLOOR), axis=0)
    gap = jnp.where(select[:, :, None], peak[:, None, :] - top[None], FLOOR)
    summed = jnp.sum(jnp.exp(gap) * total[:, None, :], axis=0)
    return top.reshape(-1), summed.reshape(-1)


def reference(src_points, tgt_points, tiles, counts):
    live_all = jnp.arange(KT, dtype=jnp.int32)[None, None, :] < counts[:, :, None]
    src_shards = src_points.reshape(PC, N_SRC, RB * TILE).transpose(1, 0, 2)
    tgt_shards = tgt_points.reshape(PC, N_TGT, CB * TILE).transpose(1, 0, 2)
    source_potential = jnp.zeros((N_SRC, RB * TILE), jnp.float32)
    target_potential = jnp.zeros((N_TGT, CB * TILE), jnp.float32)
    for sweep in range(ITERS):
        def row_shard(i):
            def row_step(carry, j):
                cost = tile_costs(src_shards[i], tgt_shards[j], tiles[i, j, 0], tiles[i, j, 1])
                picked = jnp.take(target_potential[j].reshape(CB, TILE), tiles[i, j, 1], axis=0)
                part = block_partial((picked[:, None, :] - cost) / EPS, 2, live_all[i, j], tiles[i, j, 0], RB)
                return combine(carry, part), None
            start = (jnp.full((RB * TILE,), FLOOR, jnp.float32), jnp.zeros((RB * TILE,), jnp.float32))
            (top, summed), unused = lax.scan(row_step, start, jnp.arange(N_TGT, dtype=jnp.int32))
            return EPS * jnp.log(1.0 / NS) - EPS * (top + jnp.log(summed))
        source_potential = lax.map(row_shard, jnp.arange(N_SRC, dtype=jnp.int32))

        def col_shard(j):
            def col_step(carry, i):
                cost = tile_costs(src_shards[i], tgt_shards[j], tiles[i, j, 0], tiles[i, j, 1])
                picked = jnp.take(source_potential[i].reshape(RB, TILE), tiles[i, j, 0], axis=0)
                part = block_partial((picked[:, :, None] - cost) / EPS, 1, live_all[i, j], tiles[i, j, 1], CB)
                return combine(carry, part), None
            start = (jnp.full((CB * TILE,), FLOOR, jnp.float32), jnp.zeros((CB * TILE,), jnp.float32))
            (top, summed), unused = lax.scan(col_step, start, jnp.arange(N_SRC, dtype=jnp.int32))
            return EPS * jnp.log(1.0 / NT) - EPS * (top + jnp.log(summed))
        target_potential = lax.map(col_shard, jnp.arange(N_TGT, dtype=jnp.int32))
    return source_potential.reshape(NS), target_potential.reshape(NT)
```

```python
import functools
import math

import jax
import jax.numpy as jnp
from jax import lax
from jax.experimental import pallas as pl
from jax.experimental.pallas import tpu as pltpu
from jax.sharding import PartitionSpec as P

TILE = 256
HALF = 128
ROWS = 8
ITERS = 3
EPS = 0.05
FLOOR = -1e30
SCALE = 1.0 / (EPS * math.log(2.0))
DEPTH = 64
VMEM_LIMIT = 16 * 1024 * 1024


def lse2(first, second):
    top = jnp.maximum(first, second)
    return top + jnp.log2(1.0 + jnp.exp2(jnp.minimum(first, second) - top))


def lse2_many(parts):
    top = functools.reduce(jnp.maximum, parts)
    return top + jnp.log2(functools.reduce(jnp.add, [jnp.exp2(p - top) for p in parts]))


def split(value):
    high = value.astype(jnp.bfloat16)
    rest = value - high.astype(jnp.float32)
    middle = rest.astype(jnp.bfloat16)
    low = (rest - middle.astype(jnp.float32)).astype(jnp.bfloat16)
    return high, middle, low


def cost_kernel(tiles, counts, src, tgt, cost_ab, cost_ba, xs, ys, ext, left, right, xsem, ysem):
    live = counts[0]
    width = src.shape[0]

    def copies(k):
        row = pl.multiple_of(tiles[0, k] * TILE, TILE)
        col = pl.multiple_of(tiles[1, k] * TILE, TILE)
        return (
            pltpu.make_async_copy(src.at[:, pl.ds(row, TILE)], xs.at[k], xsem.at[k]),
            pltpu.make_async_copy(tgt.at[:, pl.ds(col, TILE)], ys.at[k], ysem.at[k]),
        )

    def begin(k, carry):
        one, two = copies(k)
        one.start()
        two.start()
        return carry

    lax.fori_loop(0, live, begin, 0)
    ext[...] = jnp.zeros_like(ext)

    def step(k, carry):
        one, two = copies(k)
        one.wait()
        two.wait()
        x = xs[k]
        y = ys[k]
        ext[0, pl.ds(0, width), :] = x * (-2.0 * SCALE)
        ext[0, pl.ds(width, 1), :] = jnp.sum(x * x, axis=0, keepdims=True) * SCALE
        ext[0, pl.ds(width + 1, 1), :] = jnp.full((1, TILE), SCALE, jnp.float32)
        ext[1, pl.ds(0, width), :] = y
        ext[1, pl.ds(width, 1), :] = jnp.ones((1, TILE), jnp.float32)
        ext[1, pl.ds(width + 1, 1), :] = jnp.sum(y * y, axis=0, keepdims=True)
        xh, xm, xl = split(ext[0])
        yh, ym, yl = split(ext[1])
        for n, part in enumerate((xh, xh, xm, xm, xh, xl)):
            left[pl.ds(n * DEPTH, DEPTH), :] = part
        for n, part in enumerate((yh, ym, yh, ym, yl, yh)):
            right[pl.ds(n * DEPTH, DEPTH), :] = part
        dims = (((0,), (0,)), ((), ()))
        cost_ab[k] = lax.dot_general(left[...], right[...], dims, preferred_element_type=jnp.float32)
        cost_ba[k] = lax.dot_general(right[...], left[...], dims, preferred_element_type=jnp.float32)
        return carry

    lax.fori_loop(0, live, step, 0)


def sweep_kernel(offset, scale, inner, outer, blocks_in, blocks_out, tiles, counts, cost, *refs):
    parts = refs[:-5]
    out, result, spread, top, total = refs[-5:]
    live = counts[0]
    if parts:
        potential = offset - lse2_many([part[...] for part in parts])
        result[...] = potential * scale
        padded = potential
        if blocks_in < HALF:
            padded = jnp.concatenate(
                [potential, jnp.zeros((HALF - blocks_in, TILE), jnp.float32)], axis=0
            )
        spread[...] = padded.T
    else:
        result[...] = jnp.zeros_like(result)
    top[...] = jnp.full_like(top, FLOOR)
    total[...] = jnp.zeros_like(total)

    def column(k):
        if not parts:
            return jnp.zeros((TILE, HALF), jnp.float32)
        index = jnp.full((TILE, HALF), tiles[inner, k], jnp.int32)
        return jnp.take_along_axis(spread[...], index, axis=1, mode="promise_in_bounds")

    def scores(k, pot, h):
        return pot - cost[k, :, pl.ds(h * HALF, HALF)]

    def peaks(k, carry):
        pot = column(k)
        block = tiles[outer, k]
        for h in range(2):
            lanes = pl.ds(h * HALF, HALF)
            peak = jnp.max(scores(k, pot, h), axis=0, keepdims=True)
            top[block, :, lanes] = jnp.maximum(top[block, :, lanes], peak)
        return carry

    lax.fori_loop(0, live, peaks, 0)

    def sums(k, carry):
        pot = column(k)
        block = tiles[outer, k]
        for h in range(2):
            lanes = pl.ds(h * HALF, HALF)
            shift = top[block, pl.ds(0, 1), lanes]
            terms = jnp.exp2(scores(k, pot, h) - shift)
            part = jnp.sum(terms.reshape(TILE // ROWS, ROWS, HALF), axis=0)
            total[block, :, lanes] = total[block, :, lanes] + part
        return carry

    lax.fori_loop(0, live, sums, 0)
    summed = jnp.sum(total[...], axis=1)
    found = summed > 0.0
    out[...] = jnp.where(found, jnp.max(top[...], axis=1) + jnp.log2(jnp.where(found, summed, 1.0)), FLOOR)


def vmem_spec():
    return pl.BlockSpec(memory_space=pltpu.VMEM)


def smem_spec():
    return pl.BlockSpec(memory_space=pltpu.SMEM)


def costs(tiles, counts, src, tgt):
    slots = tiles.shape[1]
    width = src.shape[0]
    shape = pltpu.VMEM((slots, TILE, TILE), jnp.float32)
    return pl.pallas_call(
        cost_kernel,
        out_shape=(shape, shape),
        in_specs=[smem_spec(), smem_spec(), pl.BlockSpec(memory_space=pl.ANY), pl.BlockSpec(memory_space=pl.ANY)],
        out_specs=(vmem_spec(), vmem_spec()),
        scratch_shapes=[
            pltpu.VMEM((slots, width, TILE), jnp.float32),
            pltpu.VMEM((slots, width, TILE), jnp.float32),
            pltpu.VMEM((2, DEPTH, TILE), jnp.float32),
            pltpu.VMEM((6 * DEPTH, TILE), jnp.bfloat16),
            pltpu.VMEM((6 * DEPTH, TILE), jnp.bfloat16),
            pltpu.SemaphoreType.DMA((slots,)),
            pltpu.SemaphoreType.DMA((slots,)),
        ],
        compiler_params=pltpu.CompilerParams(vmem_limit_bytes=VMEM_LIMIT),
    )(tiles, counts, src, tgt)


def sweep(tiles, counts, cost, parts, cells, inner, outer, blocks_in, blocks_out):
    kernel = functools.partial(
        sweep_kernel, math.log2(1.0 / cells), 1.0 / SCALE, inner, outer, blocks_in, blocks_out
    )
    return pl.pallas_call(
        kernel,
        out_shape=(
            jax.ShapeDtypeStruct((blocks_out, TILE), jnp.float32),
            jax.ShapeDtypeStruct((blocks_in, TILE), jnp.float32),
        ),
        in_specs=[smem_spec(), smem_spec()] + [vmem_spec()] * (1 + len(parts)),
        out_specs=(vmem_spec(), vmem_spec()),
        scratch_shapes=[
            pltpu.VMEM((TILE, HALF), jnp.float32),
            pltpu.VMEM((blocks_out, ROWS, TILE), jnp.float32),
            pltpu.VMEM((blocks_out, ROWS, TILE), jnp.float32),
        ],
        compiler_params=pltpu.CompilerParams(vmem_limit_bytes=VMEM_LIMIT),
    )(tiles, counts, cost, *parts)


def fan(value, axis, size, stride, count):
    got = [value]
    for turn in range(1, count):
        pairs = []
        for k in range(size):
            place = (k // stride) % count
            pairs.append((k, k + ((place ^ turn) - place) * stride))
        got.append(lax.ppermute(value, axis, pairs))
    return got


def pair(value, axis, size, flip):
    return [value, lax.ppermute(value, axis, [(k, flip(k)) for k in range(size)])]


def over_tgt(value):
    size = lax.axis_size("tgt")
    value = lse2_many(pair(value, "tgt", size, lambda k: k ^ 1))
    return fan(value, "tgt", size, 2, size // 2)


def over_src(value):
    size = lax.axis_size("src")
    value = lse2_many(fan(value, "src", size, 1, 4))
    value = lse2_many(pair(value, "src", size, lambda k: k ^ 4))
    value = lse2_many(pair(value, "src", size, lambda k: k ^ 12))
    return pair(value, "src", size, lambda k: k ^ 28)


def body(src_points, tgt_points, tiles, counts):
    tiles = tiles[0, 0]
    counts = counts[0]
    row_blocks = src_points.shape[1] // TILE
    col_blocks = tgt_points.shape[1] // TILE
    src_cells = src_points.shape[1] * lax.axis_size("src")
    tgt_cells = tgt_points.shape[1] * lax.axis_size("tgt")
    cost_ab, cost_ba = costs(tiles, counts, src_points, tgt_points)
    parts = []
    for _ in range(ITERS):
        rows, _ = sweep(tiles, counts, cost_ba, parts, tgt_cells, 1, 0, col_blocks, row_blocks)
        parts = over_tgt(rows)
        cols, source = sweep(tiles, counts, cost_ab, parts, src_cells, 0, 1, row_blocks, col_blocks)
        parts = over_src(cols)
    target = (math.log2(1.0 / tgt_cells) - lse2_many(parts)) / SCALE
    return (source.reshape(-1), target.reshape(-1))


def solution(mesh):
    in_specs = (P(None, "src"), P(None, "tgt"), P("src", "tgt", None, None), P("src", "tgt"))
    out_specs = (P("src"), P("tgt"))
    return jax.shard_map(body, mesh=mesh, in_specs=in_specs, out_specs=out_specs, check_vma=False)
```

```python
import functools
import math

import jax
import jax.numpy as jnp
from jax import lax
from jax.experimental import pallas as pl
from jax.experimental.pallas import tpu as pltpu
from jax.sharding import PartitionSpec as P

TILE = 256
HALF = 128
ROWS = 8
GROUP = 8
ITERS = 3
EPS = 0.05
FLOOR = -1e30
SCALE = 1.0 / (EPS * math.log(2.0))
DEPTH = 64
LEAST = 2.0**-80
MOST = 2.0**100
VMEM_LIMIT = 16 * 1024 * 1024


def lse2_many(parts):
    top = functools.reduce(jnp.maximum, parts)
    return top + jnp.log2(functools.reduce(jnp.add, [jnp.exp2(p - top) for p in parts]))


def split(value):
    high = value.astype(jnp.bfloat16)
    rest = value - high.astype(jnp.float32)
    middle = rest.astype(jnp.bfloat16)
    low = (rest - middle.astype(jnp.float32)).astype(jnp.bfloat16)
    return high, middle, low


def halves():
    return [(h, pl.ds(h * HALF, HALF)) for h in range(2)]


def block(tiles, side, k, blocks):
    return jnp.minimum(tiles[side, k], blocks - 1)


def sums(k, cost, potential, shift):
    found = []
    for h, lanes in halves():
        kept = None
        for g, cells in halves():
            score = cost[k, cells, lanes]
            score = (0.0 - score if potential is None else potential[g] - score) - shift[h]
            part = jnp.sum(jnp.exp2(score).reshape(HALF // ROWS, ROWS, HALF), axis=0)
            kept = part if kept is None else kept + part
        found.append(jnp.sum(kept, axis=0, keepdims=True))
    return found


def peaks(k, cost, potential):
    found = []
    for h, lanes in halves():
        kept = None
        for g, cells in halves():
            score = cost[k, cells, lanes]
            score = 0.0 - score if potential is None else potential[g] - score
            part = jnp.max(score, axis=0, keepdims=True)
            kept = part if kept is None else jnp.maximum(kept, part)
        found.append(kept)
    return found


def spread(held, index):
    return [jnp.broadcast_to(held[g, pl.ds(index, 1), :], (HALF, HALF)).T for g in range(2)]


def add_up(live, tiles, outer, blocks_out, cost, potential_of, top, total):
    def group(q, carry):
        least, most = carry
        ready = []
        for u in range(GROUP):
            k = q * GROUP + u
            out = block(tiles, outer, k, blocks_out)
            shift = [top[h, pl.ds(out, 1), :] for h in range(2)]
            ready.append((k < live, out, sums(k, cost, potential_of(k), shift)))
        for on, out, found in ready:
            for h in range(2):
                total[h, pl.ds(out, 1), :] = total[h, pl.ds(out, 1), :] + jnp.where(on, found[h], 0.0)
                least = jnp.minimum(least, jnp.where(on, found[h], 1.0))
                most = jnp.maximum(most, jnp.where(on, found[h], 1.0))
        return least, most

    one = jnp.ones((1, HALF), jnp.float32)
    return lax.fori_loop(0, (live + GROUP - 1) // GROUP, group, (one, one))


def finish(out, top, total):
    for h, lanes in halves():
        found = total[h] > 0.0
        out[:, lanes] = jnp.where(found, top[h] + jnp.log2(jnp.where(found, total[h], 1.0)), FLOOR)


def cost_kernel(
    blocks_in, blocks_out, tiles, counts, src, tgt, cost_ab, cost_ba, out,
    xs, ys, ext, top, total, xsem, ysem
):
    live = counts[0]
    width = src.shape[0]

    def copies(k):
        row = pl.multiple_of(block(tiles, 0, k, blocks_out) * TILE, TILE)
        col = pl.multiple_of(block(tiles, 1, k, blocks_in) * TILE, TILE)
        return (
            pltpu.make_async_copy(src.at[:, pl.ds(row, TILE)], xs.at[k], xsem.at[k]),
            pltpu.make_async_copy(tgt.at[:, pl.ds(col, TILE)], ys.at[k], ysem.at[k]),
        )

    def begin(k, carry):
        for one in copies(k):
            one.start()
        return carry

    def end(k, carry):
        for one in copies(k):
            one.wait()
        return carry

    lax.fori_loop(0, live, begin, 0)
    ext[...] = jnp.zeros_like(ext)
    top[...] = jnp.full_like(top, FLOOR)
    total[...] = jnp.zeros_like(total)
    dims = (((0,), (0,)), ((), ()))

    def group(q, carry):
        lax.fori_loop(q * GROUP, jnp.minimum(live, q * GROUP + GROUP), end, 0)
        ready = []
        for u in range(GROUP):
            k = q * GROUP + u
            x = xs[k]
            y = ys[k]
            ext[u, 0, pl.ds(0, width), :] = x * (-2.0 * SCALE)
            ext[u, 0, pl.ds(width, 1), :] = jnp.sum(x * x, axis=0, keepdims=True) * SCALE
            ext[u, 0, pl.ds(width + 1, 1), :] = jnp.full((1, TILE), SCALE, jnp.float32)
            ext[u, 1, pl.ds(0, width), :] = y
            ext[u, 1, pl.ds(width, 1), :] = jnp.ones((1, TILE), jnp.float32)
            ext[u, 1, pl.ds(width + 1, 1), :] = jnp.sum(y * y, axis=0, keepdims=True)
            xh, xm, xl = split(ext[u, 0])
            yh, ym, yl = split(ext[u, 1])
            left = jnp.concatenate((xh, xh, xm, xm, xh, xl), axis=0)
            right = jnp.concatenate((yh, ym, yh, ym, yl, yh), axis=0)
            cost_ab[k] = lax.dot_general(left, right, dims, preferred_element_type=jnp.float32)
            value = lax.dot_general(right, left, dims, preferred_element_type=jnp.float32)
            cost_ba[k] = value
            peak = 0.0 - jnp.min(value, axis=0, keepdims=True)
            ready.append((k < live, block(tiles, 0, k, blocks_out), peak))
        for on, index, peak in ready:
            for h, lanes in halves():
                new = jnp.where(on, peak[:, h * HALF : (h + 1) * HALF], FLOOR)
                top[h, pl.ds(index, 1), :] = jnp.maximum(top[h, pl.ds(index, 1), :], new)
        return carry

    lax.fori_loop(0, (live + GROUP - 1) // GROUP, group, 0)
    add_up(live, tiles, 0, blocks_out, cost_ba, lambda k: None, top, total)
    finish(out, top, total)


def sweep_kernel(offset, far, scale, inner, outer, blocks_in, blocks_out, tiles, counts, cost, *refs):
    parts = refs[:-5]
    out, result, held, top, total = refs[-5:]
    live = counts[0]
    before = None
    if far is not None:
        before, parts = parts[0], parts[1:]
    potential = offset - lse2_many([part[...] for part in parts])
    result[...] = potential * scale
    for h, lanes in halves():
        held[h] = potential[:, h * HALF : (h + 1) * HALF]
        if before is None:
            top[h] = jnp.full((blocks_out, HALF), offset, jnp.float32)
        else:
            top[h] = far - before[:, lanes]
    total[...] = jnp.zeros_like(total)

    def potential_of(k):
        return spread(held, block(tiles, inner, k, blocks_in))

    least, most = add_up(live, tiles, outer, blocks_out, cost, potential_of, top, total)
    finish(out, top, total)
    exact = (jnp.min(least) >= LEAST) & (jnp.max(most) <= MOST)

    @pl.when(jnp.logical_not(exact))
    def _():
        top[...] = jnp.full_like(top, FLOOR)
        total[...] = jnp.zeros_like(total)

        def step(k, carry):
            index = block(tiles, outer, k, blocks_out)
            found = peaks(k, cost, potential_of(k))
            for h in range(2):
                top[h, pl.ds(index, 1), :] = jnp.maximum(top[h, pl.ds(index, 1), :], found[h])
            return carry

        lax.fori_loop(0, live, step, 0)
        add_up(live, tiles, outer, blocks_out, cost, potential_of, top, total)
        finish(out, top, total)


def vmem_spec():
    return pl.BlockSpec(memory_space=pltpu.VMEM)


def smem_spec():
    return pl.BlockSpec(memory_space=pltpu.SMEM)


def hbm_spec():
    return pl.BlockSpec(memory_space=pltpu.HBM)


def costs(tiles, counts, src, tgt, blocks_in, blocks_out):
    slots = tiles.shape[1]
    width = src.shape[0]
    shape = pltpu.VMEM((slots, TILE, TILE), jnp.float32)
    src = pltpu.with_memory_space_constraint(src, pltpu.HBM)
    tgt = pltpu.with_memory_space_constraint(tgt, pltpu.HBM)
    return pl.pallas_call(
        functools.partial(cost_kernel, blocks_in, blocks_out),
        out_shape=(shape, shape, jax.ShapeDtypeStruct((blocks_out, TILE), jnp.float32)),
        in_specs=[smem_spec(), smem_spec(), hbm_spec(), hbm_spec()],
        out_specs=(vmem_spec(), vmem_spec(), vmem_spec()),
        scratch_shapes=[
            pltpu.VMEM((slots, width, TILE), jnp.float32),
            pltpu.VMEM((slots, width, TILE), jnp.float32),
            pltpu.VMEM((GROUP, 2, DEPTH, TILE), jnp.float32),
            pltpu.VMEM((2, blocks_out, HALF), jnp.float32),
            pltpu.VMEM((2, blocks_out, HALF), jnp.float32),
            pltpu.SemaphoreType.DMA((slots,)),
            pltpu.SemaphoreType.DMA((slots,)),
        ],
        compiler_params=pltpu.CompilerParams(vmem_limit_bytes=VMEM_LIMIT),
    )(tiles, counts, src, tgt)


def sweep(tiles, counts, cost, before, parts, cells, far_cells, inner, outer, blocks_in, blocks_out, scale):
    far = None if before is None else math.log2(1.0 / far_cells)
    operands = list(parts) if before is None else [before, *parts]
    kernel = functools.partial(
        sweep_kernel, math.log2(1.0 / cells), far, scale, inner, outer, blocks_in, blocks_out
    )
    return pl.pallas_call(
        kernel,
        out_shape=(
            jax.ShapeDtypeStruct((blocks_out, TILE), jnp.float32),
            jax.ShapeDtypeStruct((blocks_in, TILE), jnp.float32),
        ),
        in_specs=[smem_spec(), smem_spec()] + [vmem_spec()] * (1 + len(operands)),
        out_specs=(vmem_spec(), vmem_spec()),
        scratch_shapes=[
            pltpu.VMEM((2, blocks_in, HALF), jnp.float32),
            pltpu.VMEM((2, blocks_out, HALF), jnp.float32),
            pltpu.VMEM((2, blocks_out, HALF), jnp.float32),
        ],
        compiler_params=pltpu.CompilerParams(vmem_limit_bytes=VMEM_LIMIT),
    )(tiles, counts, cost, *operands)


def fan(value, axis, size, stride, count):
    got = [value]
    for turn in range(1, count):
        pairs = []
        for k in range(size):
            place = (k // stride) % count
            pairs.append((k, k + ((place ^ turn) - place) * stride))
        got.append(lax.ppermute(value, axis, pairs))
    return got


def pair(value, axis, size, flip):
    return [value, lax.ppermute(value, axis, [(k, flip(k)) for k in range(size)])]


def over_tgt(value):
    size = lax.axis_size("tgt")
    value = lse2_many(pair(value, "tgt", size, lambda k: k ^ 1))
    return fan(value, "tgt", size, 2, size // 2)


def over_src(value):
    size = lax.axis_size("src")
    value = lse2_many(fan(value, "src", size, 1, 4))
    value = lse2_many(pair(value, "src", size, lambda k: k ^ 4))
    value = lse2_many(pair(value, "src", size, lambda k: k ^ 12))
    return pair(value, "src", size, lambda k: k ^ 28)


def body(src_points, tgt_points, tiles, counts):
    tiles = tiles[0, 0]
    counts = counts[0]
    row_blocks = src_points.shape[1] // TILE
    col_blocks = tgt_points.shape[1] // TILE
    src_cells = src_points.shape[1] * lax.axis_size("src")
    tgt_cells = tgt_points.shape[1] * lax.axis_size("tgt")
    cost_ab, cost_ba, rows = costs(tiles, counts, src_points, tgt_points, col_blocks, row_blocks)
    target = None
    for turn in range(ITERS):
        last = turn == ITERS - 1
        cols, source = sweep(
            tiles, counts, cost_ab, target, over_tgt(rows), src_cells, tgt_cells, 0, 1,
            row_blocks, col_blocks, 1.0 / SCALE if last else 1.0,
        )
        parts = over_src(cols)
        if last:
            target = (math.log2(1.0 / tgt_cells) - lse2_many(parts)) / SCALE
        else:
            rows, target = sweep(
                tiles, counts, cost_ba, source, parts, tgt_cells, src_cells, 1, 0,
                col_blocks, row_blocks, 1.0,
            )
    return (source.reshape(-1), target.reshape(-1))


def solution(mesh):
    in_specs = (P(None, "src"), P(None, "tgt"), P("src", "tgt", None, None), P("src", "tgt"))
    out_specs = (P("src"), P("tgt"))
    return jax.shard_map(body, mesh=mesh, in_specs=in_specs, out_specs=out_specs, check_vma=False)
```

```python
import functools
import math

import jax
import jax.numpy as jnp
from jax import lax
from jax.experimental import pallas as pl
from jax.experimental.pallas import tpu as pltpu
from jax.sharding import PartitionSpec as P

TILE = 256
HALF = 128
ROWS = 8
GROUP = 8
ITERS = 3
EPS = 0.05
FLOOR = -1e30
SCALE = 1.0 / (EPS * math.log(2.0))
DEPTH = 64
LEAST = 2.0**-80
MOST = 2.0**100
VMEM_LIMIT = 16 * 1024 * 1024


def lse2_many(parts):
    top = functools.reduce(jnp.maximum, parts)
    return top + jnp.log2(functools.reduce(jnp.add, [jnp.exp2(p - top) for p in parts]))


def split(value):
    high = value.astype(jnp.bfloat16)
    return high, (value - high.astype(jnp.float32)).astype(jnp.bfloat16)


def halves():
    return [(h, pl.ds(h * HALF, HALF)) for h in range(2)]


def row(index, h):
    return pl.ds(2 * index + h, 1)


def block(tiles, side, k, blocks):
    return jnp.minimum(tiles[side, k], blocks - 1)


def sums(k, cost, potential, shift):
    found = []
    for h, lanes in halves():
        kept = None
        for g, cells in halves():
            score = cost[k, cells, lanes]
            score = (0.0 - score if potential is None else potential[g] - score) - shift[h]
            part = jnp.sum(jnp.exp2(score).reshape(HALF // ROWS, ROWS, HALF), axis=0)
            kept = part if kept is None else kept + part
        found.append(jnp.sum(kept, axis=0, keepdims=True))
    return found


def peaks(k, cost, potential):
    found = []
    for h, lanes in halves():
        kept = None
        for g, cells in halves():
            score = cost[k, cells, lanes]
            score = 0.0 - score if potential is None else potential[g] - score
            part = jnp.max(score, axis=0, keepdims=True)
            kept = part if kept is None else jnp.maximum(kept, part)
        found.append(kept)
    return found


def spread(held, index):
    return [jnp.broadcast_to(held[row(index, g), :], (HALF, HALF)).T for g in range(2)]


def add_up(live, tiles, outer, blocks_out, cost, potential_of, top, total):
    def group(q, carry):
        least, most = carry
        ready = []
        for u in range(GROUP):
            k = q * GROUP + u
            out = block(tiles, outer, k, blocks_out)
            shift = [top[row(out, h), :] for h in range(2)]
            ready.append((k < live, out, sums(k, cost, potential_of(k), shift)))
        for on, out, found in ready:
            for h in range(2):
                total[row(out, h), :] = total[row(out, h), :] + jnp.where(on, found[h], 0.0)
                least = jnp.minimum(least, jnp.where(on, found[h], 1.0))
                most = jnp.maximum(most, jnp.where(on, found[h], 1.0))
        return least, most

    one = jnp.ones((1, HALF), jnp.float32)
    return lax.fori_loop(0, (live + GROUP - 1) // GROUP, group, (one, one))


def finish(out, top, total):
    found = total[...] > 0.0
    out[...] = jnp.where(found, top[...] + jnp.log2(jnp.where(found, total[...], 1.0)), FLOOR)


def table_scratch(slots):
    return [pltpu.SMEM((2, slots), jnp.int32), pltpu.SemaphoreType.DMA(())]


def cost_kernel(
    blocks_in, blocks_out, tiles_in, counts, src, tgt, cost_ab, cost_ba, out,
    tiles, tsem, xs, ys, ext, top, total, xsem, ysem
):
    table = pltpu.make_async_copy(tiles_in, tiles, tsem)
    table.start()
    table.wait()
    live = counts[0, 0]
    width = src.shape[0]

    def copies(k):
        first = pl.multiple_of(block(tiles, 0, k, blocks_out) * TILE, TILE)
        second = pl.multiple_of(block(tiles, 1, k, blocks_in) * TILE, TILE)
        return (
            pltpu.make_async_copy(src.at[:, pl.ds(first, TILE)], xs.at[k], xsem.at[k]),
            pltpu.make_async_copy(tgt.at[:, pl.ds(second, TILE)], ys.at[k], ysem.at[k]),
        )

    def begin(k, carry):
        for one in copies(k):
            one.start()
        return carry

    def end(k, carry):
        for one in copies(k):
            one.wait()
        return carry

    lax.fori_loop(0, live, begin, 0)
    ext[...] = jnp.zeros_like(ext)
    for u in range(GROUP):
        for side, place in ((0, 1), (0, 3), (1, 0), (1, 2)):
            ext[u, side, pl.ds(width + place, 1), :] = jnp.ones((1, TILE), jnp.float32)
    top[...] = jnp.full_like(top, FLOOR)
    total[...] = jnp.zeros_like(total)

    def extend(u, side, points, scale):
        square = jnp.sum(points * points, axis=0, keepdims=True) * SCALE
        high, middle = split(square)
        ext[u, side, pl.ds(0, width), :] = points * scale
        ext[u, side, pl.ds(width + side, 1), :] = square
        rest = square - high.astype(jnp.float32) - middle.astype(jnp.float32)
        ext[u, side, pl.ds(width + side + 2, 1), :] = rest
        return split(ext[u, side])

    def product(first, second):
        turned = jnp.concatenate(first, axis=0).T
        turned = jnp.concatenate((turned, turned), axis=1)
        high, middle = second
        other = jnp.concatenate((high, high, middle, middle), axis=0)
        return jnp.dot(turned, other, preferred_element_type=jnp.float32)

    def group(q, carry):
        lax.fori_loop(q * GROUP, jnp.minimum(live, q * GROUP + GROUP), end, 0)
        ready = []
        for u in range(GROUP):
            k = q * GROUP + u
            centre = ys[k, :, pl.ds(0, 1)]
            left = extend(u, 0, xs[k] - centre, -2.0 * SCALE)
            right = extend(u, 1, ys[k] - centre, 1.0)
            cost_ab[k] = product(left, right)
            value = product(right, left)
            cost_ba[k] = value
            peak = 0.0 - jnp.min(value, axis=0, keepdims=True)
            ready.append((k < live, block(tiles, 0, k, blocks_out), peak))
        for on, index, peak in ready:
            for h in range(2):
                new = jnp.where(on, peak[:, h * HALF : (h + 1) * HALF], FLOOR)
                top[row(index, h), :] = jnp.maximum(top[row(index, h), :], new)
        return carry

    lax.fori_loop(0, (live + GROUP - 1) // GROUP, group, 0)
    add_up(live, tiles, 0, blocks_out, cost_ba, lambda k: None, top, total)
    finish(out, top, total)


def sweep_kernel(offset, far, scale, inner, outer, blocks_in, blocks_out, tiles_in, counts, cost, *refs):
    parts = refs[:-7]
    out, result, tiles, tsem, held, top, total = refs[-7:]
    table = pltpu.make_async_copy(tiles_in, tiles, tsem)
    table.start()
    if far is None:
        top[...] = jnp.full_like(top, offset)
    else:
        top[...] = far - parts[0][...]
        parts = parts[1:]
    potential = offset - lse2_many([part[...] for part in parts])
    result[...] = potential * scale
    held[...] = potential
    total[...] = jnp.zeros_like(total)
    table.wait()
    live = counts[0, 0]

    def potential_of(k):
        return spread(held, block(tiles, inner, k, blocks_in))

    least, most = add_up(live, tiles, outer, blocks_out, cost, potential_of, top, total)
    finish(out, top, total)
    exact = (jnp.min(least) >= LEAST) & (jnp.max(most) <= MOST)

    @pl.when(jnp.logical_not(exact))
    def _():
        top[...] = jnp.full_like(top, FLOOR)
        total[...] = jnp.zeros_like(total)

        def step(k, carry):
            index = block(tiles, outer, k, blocks_out)
            found = peaks(k, cost, potential_of(k))
            for h in range(2):
                top[row(index, h), :] = jnp.maximum(top[row(index, h), :], found[h])
            return carry

        lax.fori_loop(0, live, step, 0)
        add_up(live, tiles, outer, blocks_out, cost, potential_of, top, total)
        finish(out, top, total)


def vmem_spec():
    return pl.BlockSpec(memory_space=pltpu.VMEM)


def smem_spec():
    return pl.BlockSpec(memory_space=pltpu.SMEM)


def hbm_spec():
    return pl.BlockSpec(memory_space=pltpu.HBM)


def costs(tiles, counts, src, tgt, blocks_in, blocks_out):
    slots = tiles.shape[1]
    width = src.shape[0]
    shape = pltpu.VMEM((slots, TILE, TILE), jnp.float32)
    return pl.pallas_call(
        functools.partial(cost_kernel, blocks_in, blocks_out),
        out_shape=(shape, shape, jax.ShapeDtypeStruct((2 * blocks_out, HALF), jnp.float32)),
        in_specs=[hbm_spec(), smem_spec(), hbm_spec(), hbm_spec()],
        out_specs=(vmem_spec(), vmem_spec(), vmem_spec()),
        scratch_shapes=[
            *table_scratch(slots),
            pltpu.VMEM((slots, width, TILE), jnp.float32),
            pltpu.VMEM((slots, width, TILE), jnp.float32),
            pltpu.VMEM((GROUP, 2, DEPTH, TILE), jnp.float32),
            pltpu.VMEM((2 * blocks_out, HALF), jnp.float32),
            pltpu.VMEM((2 * blocks_out, HALF), jnp.float32),
            pltpu.SemaphoreType.DMA((slots,)),
            pltpu.SemaphoreType.DMA((slots,)),
        ],
        compiler_params=pltpu.CompilerParams(vmem_limit_bytes=VMEM_LIMIT),
    )(tiles, counts, src, tgt)


def sweep(tiles, counts, cost, before, parts, cells, far_cells, inner, outer, blocks_in, blocks_out, scale):
    far = None if before is None else math.log2(1.0 / far_cells)
    operands = list(parts) if before is None else [before, *parts]
    kernel = functools.partial(
        sweep_kernel, math.log2(1.0 / cells), far, scale, inner, outer, blocks_in, blocks_out
    )
    return pl.pallas_call(
        kernel,
        out_shape=(
            jax.ShapeDtypeStruct((2 * blocks_out, HALF), jnp.float32),
            jax.ShapeDtypeStruct((2 * blocks_in, HALF), jnp.float32),
        ),
        in_specs=[hbm_spec(), smem_spec()] + [vmem_spec()] * (1 + len(operands)),
        out_specs=(vmem_spec(), vmem_spec()),
        scratch_shapes=[
            *table_scratch(tiles.shape[1]),
            pltpu.VMEM((2 * blocks_in, HALF), jnp.float32),
            pltpu.VMEM((2 * blocks_out, HALF), jnp.float32),
            pltpu.VMEM((2 * blocks_out, HALF), jnp.float32),
        ],
        compiler_params=pltpu.CompilerParams(vmem_limit_bytes=VMEM_LIMIT),
    )(tiles, counts, cost, *operands)


def fan(value, axis, size, stride, count):
    got = [value]
    for turn in range(1, count):
        pairs = []
        for k in range(size):
            place = (k // stride) % count
            pairs.append((k, k + ((place ^ turn) - place) * stride))
        got.append(lax.ppermute(value, axis, pairs))
    return got


def pair(value, axis, size, flip):
    return [value, lax.ppermute(value, axis, [(k, flip(k)) for k in range(size)])]


def over_tgt(value):
    size = lax.axis_size("tgt")
    value = lse2_many(pair(value, "tgt", size, lambda k: k ^ 1))
    return fan(value, "tgt", size, 2, size // 2)


def over_src(value):
    size = lax.axis_size("src")
    value = lse2_many(fan(value, "src", size, 1, 4))
    value = lse2_many(pair(value, "src", size, lambda k: k ^ 4))
    value = lse2_many(pair(value, "src", size, lambda k: k ^ 12))
    return pair(value, "src", size, lambda k: k ^ 28)


def body(src_points, tgt_points, tiles, counts):
    tiles, src_points, tgt_points = (
        pltpu.with_memory_space_constraint(each, pltpu.HBM)
        for each in (tiles[0, 0], src_points, tgt_points)
    )
    row_blocks = src_points.shape[1] // TILE
    col_blocks = tgt_points.shape[1] // TILE
    src_cells = src_points.shape[1] * lax.axis_size("src")
    tgt_cells = tgt_points.shape[1] * lax.axis_size("tgt")
    cost_ab, cost_ba, rows = costs(tiles, counts, src_points, tgt_points, col_blocks, row_blocks)
    target = None
    for turn in range(ITERS):
        last = turn == ITERS - 1
        cols, source = sweep(
            tiles, counts, cost_ab, target, over_tgt(rows), src_cells, tgt_cells, 0, 1,
            row_blocks, col_blocks, 1.0 / SCALE if last else 1.0,
        )
        parts = over_src(cols)
        if last:
            target = (math.log2(1.0 / tgt_cells) - lse2_many(parts)) / SCALE
        else:
            rows, target = sweep(
                tiles, counts, cost_ba, source, parts, tgt_cells, src_cells, 1, 0,
                col_blocks, row_blocks, 1.0,
            )
    return (source.reshape(-1), target.reshape(-1))


def solution(mesh):
    in_specs = (P(None, "src"), P(None, "tgt"), P("src", "tgt", None, None), P("src", "tgt"))
    out_specs = (P("src"), P("tgt"))
    return jax.shard_map(body, mesh=mesh, in_specs=in_specs, out_specs=out_specs, check_vma=False)
```

```python
import functools
import math

import jax
import jax.numpy as jnp
from jax import lax
from jax.experimental import pallas as pl
from jax.experimental.pallas import tpu as pltpu
from jax.sharding import PartitionSpec as P

TILE = 256
HALF = 128
ROWS = 8
GROUP = 8
WIDE = 16
ITERS = 3
EPS = 0.05
FLOOR = -1e30
SCALE = 1.0 / (EPS * math.log(2.0))
DEPTH = 64
LEAST = 2.0**-80
MOST = 2.0**100
VMEM_LIMIT = 16 * 1024 * 1024


def lse2_many(parts):
    top = functools.reduce(jnp.maximum, parts)
    return top + jnp.log2(functools.reduce(jnp.add, [jnp.exp2(p - top) for p in parts]))


def split(value):
    high = value.astype(jnp.bfloat16)
    return high, (value - high.astype(jnp.float32)).astype(jnp.bfloat16)


def halves():
    return [(h, pl.ds(h * HALF, HALF)) for h in range(2)]


def row(index, h):
    return pl.ds(2 * index + h, 1)


def block(tiles, side, k, blocks):
    return jnp.minimum(tiles[side, k], blocks - 1)


def sums(k, cost, potential, shift):
    found = []
    for h, lanes in halves():
        kept = None
        for g, cells in halves():
            score = cost[k, cells, lanes]
            score = (0.0 - score if potential is None else potential[g] - score) - shift[h]
            part = jnp.sum(jnp.exp2(score).reshape(HALF // ROWS, ROWS, HALF), axis=0)
            kept = part if kept is None else kept + part
        found.append(jnp.sum(kept, axis=0, keepdims=True))
    return found


def peaks(k, cost, potential):
    found = []
    for h, lanes in halves():
        kept = None
        for g, cells in halves():
            score = cost[k, cells, lanes]
            score = 0.0 - score if potential is None else potential[g] - score
            part = jnp.max(score, axis=0, keepdims=True)
            kept = part if kept is None else jnp.maximum(kept, part)
        found.append(kept)
    return found


def spread(held, index):
    return [jnp.broadcast_to(held[0, row(index, g), :], (HALF, HALF)).T for g in range(2)]


def add_up(size, live, tiles, outer, blocks_out, cost, potential_of, top, total):
    def group(q, carry):
        least, most = carry
        ready = []
        for u in range(size):
            k = q * size + u
            out = block(tiles, outer, k, blocks_out)
            shift = [top[row(out, h), :] for h in range(2)]
            ready.append((k < live, out, sums(k, cost, potential_of(k), shift)))
        for on, out, found in ready:
            for h in range(2):
                total[row(out, h), :] = total[row(out, h), :] + jnp.where(on, found[h], 0.0)
                least = jnp.minimum(least, jnp.where(on, found[h], 1.0))
                most = jnp.maximum(most, jnp.where(on, found[h], 1.0))
        return least, most

    one = jnp.ones((1, HALF), jnp.float32)
    return lax.fori_loop(0, (live + size - 1) // size, group, (one, one))


def finish(out, top, total):
    found = total[...] > 0.0
    out[...] = jnp.where(found, top[...] + jnp.log2(jnp.where(found, total[...], 1.0)), FLOOR)


def product(first, second):
    turned = first.T
    turned = jnp.concatenate((turned, turned), axis=1)
    high, middle = second[:DEPTH], second[DEPTH:]
    other = jnp.concatenate((high, high, middle, middle), axis=0)
    return jnp.dot(turned, other, preferred_element_type=jnp.float32)


def cost_kernel(
    blocks_in, blocks_out, tiles_in, counts, src, tgt, cost, out, lefts, rights, tiles,
    tsem, xs, ys, ext, top, total, xsem, ysem
):
    table = pltpu.make_async_copy(tiles_in, tiles, tsem)
    table.start()
    table.wait()
    live = counts[0, 0]
    width = src.shape[0]

    def copies(k):
        first = pl.multiple_of(block(tiles, 0, k, blocks_out) * TILE, TILE)
        second = pl.multiple_of(block(tiles, 1, k, blocks_in) * TILE, TILE)
        return (
            pltpu.make_async_copy(src.at[:, pl.ds(first, TILE)], xs.at[k], xsem.at[k]),
            pltpu.make_async_copy(tgt.at[:, pl.ds(second, TILE)], ys.at[k], ysem.at[k]),
        )

    def begin(k, carry):
        for one in copies(k):
            one.start()
        return carry

    def end(k, carry):
        for one in copies(k):
            one.wait()
        return carry

    lax.fori_loop(0, live, begin, 0)
    ext[...] = jnp.zeros_like(ext)
    for u in range(GROUP):
        for side, place in ((0, 1), (0, 3), (1, 0), (1, 2)):
            ext[u, side, pl.ds(width + place, 1), :] = jnp.ones((1, TILE), jnp.float32)
    top[...] = jnp.full_like(top, FLOOR)
    total[...] = jnp.zeros_like(total)

    def extend(u, side, points, scale):
        square = jnp.sum(points * points, axis=0, keepdims=True) * SCALE
        high, middle = split(square)
        ext[u, side, pl.ds(0, width), :] = points * scale
        ext[u, side, pl.ds(width + side, 1), :] = square
        rest = square - high.astype(jnp.float32) - middle.astype(jnp.float32)
        ext[u, side, pl.ds(width + side + 2, 1), :] = rest
        return jnp.concatenate(split(ext[u, side]), axis=0)

    def group(q, carry):
        lax.fori_loop(q * GROUP, jnp.minimum(live, q * GROUP + GROUP), end, 0)
        ready = []
        for u in range(GROUP):
            k = q * GROUP + u
            centre = ys[k, :, pl.ds(0, 1)]
            left = extend(u, 0, xs[k] - centre, -2.0 * SCALE)
            right = extend(u, 1, ys[k] - centre, 1.0)
            lefts[k] = left
            rights[k] = right
            value = product(right, left)
            cost[k] = value
            peak = 0.0 - jnp.min(value, axis=0, keepdims=True)
            ready.append((k < live, block(tiles, 0, k, blocks_out), peak))
        for on, index, peak in ready:
            for h in range(2):
                new = jnp.where(on, peak[:, h * HALF : (h + 1) * HALF], FLOOR)
                top[row(index, h), :] = jnp.maximum(top[row(index, h), :], new)
        return carry

    lax.fori_loop(0, (live + GROUP - 1) // GROUP, group, 0)
    add_up(GROUP, live, tiles, 0, blocks_out, cost, lambda k: None, top, total)
    finish(out, top, total)


def turn_kernel(counts, lefts, rights, cost):
    live = counts[0, 0]

    def group(q, carry):
        for u in range(GROUP):
            k = q * GROUP + u
            cost[k] = product(lefts[k], rights[k])
        return carry

    lax.fori_loop(0, (live + GROUP - 1) // GROUP, group, 0)


def sweep_kernel(offset, far, last, inner, outer, blocks_in, blocks_out, tiles, counts, cost, *refs):
    parts = refs[:-6]
    out, result, held, top, total, rsem = refs[-6:]
    if far is None:
        top[...] = jnp.full_like(top, offset)
    else:
        top[...] = far - parts[0][...]
        parts = parts[1:]
    potential = offset - lse2_many([part[...] for part in parts])
    held[0] = potential
    if last:
        held[1] = potential / SCALE
        leave = pltpu.make_async_copy(held.at[1], result, rsem)
        leave.start()
    else:
        result[...] = potential
    total[...] = jnp.zeros_like(total)
    live = counts[0, 0]

    def potential_of(k):
        return spread(held, block(tiles, inner, k, blocks_in))

    least, most = add_up(WIDE, live, tiles, outer, blocks_out, cost, potential_of, top, total)
    finish(out, top, total)
    exact = (jnp.min(least) >= LEAST) & (jnp.max(most) <= MOST)

    @pl.when(jnp.logical_not(exact))
    def _():
        top[...] = jnp.full_like(top, FLOOR)
        total[...] = jnp.zeros_like(total)

        def step(k, carry):
            index = block(tiles, outer, k, blocks_out)
            found = peaks(k, cost, potential_of(k))
            for h in range(2):
                top[row(index, h), :] = jnp.maximum(top[row(index, h), :], found[h])
            return carry

        lax.fori_loop(0, live, step, 0)
        add_up(2, live, tiles, outer, blocks_out, cost, potential_of, top, total)
        finish(out, top, total)

    if last:
        leave.wait()


def vmem_spec():
    return pl.BlockSpec(memory_space=pltpu.VMEM)


def smem_spec():
    return pl.BlockSpec(memory_space=pltpu.SMEM)


def hbm_spec():
    return pl.BlockSpec(memory_space=pltpu.HBM)


def costs(tiles, counts, src, tgt, blocks_in, blocks_out):
    slots = tiles.shape[1]
    width = src.shape[0]
    part = pltpu.VMEM((slots, 2 * DEPTH, TILE), jnp.bfloat16)
    return pl.pallas_call(
        functools.partial(cost_kernel, blocks_in, blocks_out),
        out_shape=(
            pltpu.VMEM((slots, TILE, TILE), jnp.float32),
            jax.ShapeDtypeStruct((2 * blocks_out, HALF), jnp.float32),
            part,
            part,
            pltpu.SMEM(tiles.shape, jnp.int32),
        ),
        in_specs=[hbm_spec(), smem_spec(), hbm_spec(), hbm_spec()],
        out_specs=(vmem_spec(), vmem_spec(), vmem_spec(), vmem_spec(), smem_spec()),
        scratch_shapes=[
            pltpu.SemaphoreType.DMA(()),
            pltpu.VMEM((slots, width, TILE), jnp.float32),
            pltpu.VMEM((slots, width, TILE), jnp.float32),
            pltpu.VMEM((GROUP, 2, DEPTH, TILE), jnp.float32),
            pltpu.VMEM((2 * blocks_out, HALF), jnp.float32),
            pltpu.VMEM((2 * blocks_out, HALF), jnp.float32),
            pltpu.SemaphoreType.DMA((slots,)),
            pltpu.SemaphoreType.DMA((slots,)),
        ],
        compiler_params=pltpu.CompilerParams(vmem_limit_bytes=VMEM_LIMIT),
    )(tiles, counts, src, tgt)


def turned(counts, lefts, rights):
    slots = lefts.shape[0]
    return pl.pallas_call(
        turn_kernel,
        out_shape=pltpu.VMEM((slots, TILE, TILE), jnp.float32),
        in_specs=[smem_spec(), vmem_spec(), vmem_spec()],
        out_specs=vmem_spec(),
        compiler_params=pltpu.CompilerParams(vmem_limit_bytes=VMEM_LIMIT),
        cost_estimate=pl.CostEstimate(
            flops=slots * 8 * DEPTH * TILE * TILE, bytes_accessed=slots * 8 * TILE * TILE, transcendentals=0
        ),
    )(counts, lefts, rights)


def sweep(tiles, counts, cost, before, parts, cells, far_cells, inner, outer, blocks_in, blocks_out, last):
    far = None if before is None else math.log2(1.0 / far_cells)
    operands = list(parts) if before is None else [before, *parts]
    kernel = functools.partial(
        sweep_kernel, math.log2(1.0 / cells), far, last, inner, outer, blocks_in, blocks_out
    )
    return pl.pallas_call(
        kernel,
        out_shape=(
            jax.ShapeDtypeStruct((2 * blocks_out, HALF), jnp.float32),
            jax.ShapeDtypeStruct((2 * blocks_in, HALF), jnp.float32),
        ),
        in_specs=[smem_spec(), smem_spec()] + [vmem_spec()] * (1 + len(operands)),
        out_specs=(vmem_spec(), hbm_spec() if last else vmem_spec()),
        scratch_shapes=[
            pltpu.VMEM((2, 2 * blocks_in, HALF), jnp.float32),
            pltpu.VMEM((2 * blocks_out, HALF), jnp.float32),
            pltpu.VMEM((2 * blocks_out, HALF), jnp.float32),
            pltpu.SemaphoreType.DMA(()),
        ],
        compiler_params=pltpu.CompilerParams(vmem_limit_bytes=VMEM_LIMIT),
    )(tiles, counts, cost, *operands)


def fan(value, axis, size, stride, count):
    got = [value]
    for turn in range(1, count):
        pairs = []
        for k in range(size):
            place = (k // stride) % count
            pairs.append((k, k + ((place ^ turn) - place) * stride))
        got.append(lax.ppermute(value, axis, pairs))
    return got


def pair(value, axis, size, flip):
    return [value, lax.ppermute(value, axis, [(k, flip(k)) for k in range(size)])]


def over_core(value):
    size = lax.axis_size("tgt")
    return lse2_many(pair(value, "tgt", size, lambda k: k ^ 1))


def over_y(value):
    size = lax.axis_size("tgt")
    return fan(value, "tgt", size, 2, size // 2)


def over_src(value):
    size = lax.axis_size("src")
    value = lse2_many(fan(value, "src", size, 1, 4))
    value = lse2_many(fan(value, "src", size, 4, 4))
    return pair(value, "src", size, lambda k: k ^ 28)


def body(src_points, tgt_points, tiles, counts):
    tiles, src_points, tgt_points = (
        pltpu.with_memory_space_constraint(each, pltpu.HBM)
        for each in (tiles[0, 0], src_points, tgt_points)
    )
    row_blocks = src_points.shape[1] // TILE
    col_blocks = tgt_points.shape[1] // TILE
    src_cells = src_points.shape[1] * lax.axis_size("src")
    tgt_cells = tgt_points.shape[1] * lax.axis_size("tgt")
    cost_ba, rows, lefts, rights, tiles = costs(
        tiles, counts, src_points, tgt_points, col_blocks, row_blocks
    )
    target = None
    for turn in range(ITERS):
        last = turn == ITERS - 1
        rows = over_core(rows)
        if turn == 0:
            rows, lefts = lax.optimization_barrier((rows, lefts))
            cost_ab = turned(counts, lefts, rights)
        cols, source = sweep(
            tiles, counts, cost_ab, target, over_y(rows), src_cells, tgt_cells, 0, 1,
            row_blocks, col_blocks, last,
        )
        parts = over_src(cols)
        if last:
            target = (math.log2(1.0 / tgt_cells) - lse2_many(parts)) / SCALE
        else:
            rows, target = sweep(
                tiles, counts, cost_ba, source, parts, tgt_cells, src_cells, 1, 0,
                col_blocks, row_blocks, False,
            )
    return (source.reshape(-1), target.reshape(-1))


def solution(mesh):
    in_specs = (P(None, "src"), P(None, "tgt"), P("src", "tgt", None, None), P("src", "tgt"))
    out_specs = (P("src"), P("tgt"))
    return jax.shard_map(body, mesh=mesh, in_specs=in_specs, out_specs=out_specs, check_vma=False)
```

```python
import functools
import math

import jax
import jax.numpy as jnp
from jax import lax
from jax.experimental import pallas as pl
from jax.experimental.pallas import tpu as pltpu
from jax.sharding import PartitionSpec as P

TILE = 256
HALF = 128
ROWS = 8
GROUP = 8
WIDE = 16
ITERS = 3
EPS = 0.05
FLOOR = -1e30
SCALE = 1.0 / (EPS * math.log(2.0))
DEPTH = 64
LEAST = 2.0**-80
MOST = 2.0**100
VMEM_LIMIT = 16 * 1024 * 1024


def lse2_many(parts):
    top = functools.reduce(jnp.maximum, parts)
    return top + jnp.log2(functools.reduce(jnp.add, [jnp.exp2(p - top) for p in parts]))


def split(value):
    high = value.astype(jnp.bfloat16)
    return high, (value - high.astype(jnp.float32)).astype(jnp.bfloat16)


def halves():
    return [(h, pl.ds(h * HALF, HALF)) for h in range(2)]


def row(index, h):
    return pl.ds(2 * index + h, 1)


def block(tiles, side, k, blocks):
    return jnp.minimum(tiles[side, k], blocks - 1)


def sums(k, cost, potential, shift):
    found = []
    for h, lanes in halves():
        kept = None
        for g, cells in halves():
            score = cost[k, cells, lanes]
            score = (0.0 - score if potential is None else potential[g] - score) - shift[h]
            part = jnp.sum(jnp.exp2(score).reshape(HALF // ROWS, ROWS, HALF), axis=0)
            kept = part if kept is None else kept + part
        found.append(jnp.sum(kept, axis=0, keepdims=True))
    return found


def peaks(k, cost, potential):
    found = []
    for h, lanes in halves():
        kept = None
        for g, cells in halves():
            score = cost[k, cells, lanes]
            score = 0.0 - score if potential is None else potential[g] - score
            part = jnp.max(score, axis=0, keepdims=True)
            kept = part if kept is None else jnp.maximum(kept, part)
        found.append(kept)
    return found


def spread(held, index):
    return [jnp.broadcast_to(held[0, row(index, g), :], (HALF, HALF)).T for g in range(2)]


def add_up(size, live, tiles, outer, blocks_out, cost, potential_of, top, total):
    def group(q, carry):
        least, most = carry
        ready = []
        for u in range(size):
            k = q * size + u
            out = block(tiles, outer, k, blocks_out)
            shift = [top[row(out, h), :] for h in range(2)]
            ready.append((k < live, out, sums(k, cost, potential_of(k), shift)))
        for on, out, found in ready:
            for h in range(2):
                total[row(out, h), :] = total[row(out, h), :] + jnp.where(on, found[h], 0.0)
                least = jnp.minimum(least, jnp.where(on, found[h], 1.0))
                most = jnp.maximum(most, jnp.where(on, found[h], 1.0))
        return least, most

    one = jnp.ones((1, HALF), jnp.float32)
    return lax.fori_loop(0, (live + size - 1) // size, group, (one, one))


def finish(out, top, total):
    found = total[...] > 0.0
    out[...] = jnp.where(found, top[...] + jnp.log2(jnp.where(found, total[...], 1.0)), FLOOR)


def product(first, second):
    turned = first.T
    turned = jnp.concatenate((turned, turned), axis=1)
    high, middle = second[:DEPTH], second[DEPTH:]
    other = jnp.concatenate((high, high, middle, middle), axis=0)
    return jnp.dot(turned, other, preferred_element_type=jnp.float32)


def cost_kernel(
    blocks_in, blocks_out, tiles_in, counts, src, tgt, cost, out, lefts, rights, tiles,
    tsem, xs, ys, ext, top, total, xsem, ysem
):
    table = pltpu.make_async_copy(tiles_in, tiles, tsem)
    table.start()
    table.wait()
    live = counts[0, 0]
    width = src.shape[0]

    def copies(k):
        first = pl.multiple_of(block(tiles, 0, k, blocks_out) * TILE, TILE)
        second = pl.multiple_of(block(tiles, 1, k, blocks_in) * TILE, TILE)
        return (
            pltpu.make_async_copy(src.at[:, pl.ds(first, TILE)], xs.at[k], xsem.at[k]),
            pltpu.make_async_copy(tgt.at[:, pl.ds(second, TILE)], ys.at[k], ysem.at[k]),
        )

    def begin(k, carry):
        for one in copies(k):
            one.start()
        return carry

    def end(k, carry):
        for one in copies(k):
            one.wait()
        return carry

    lax.fori_loop(0, live, begin, 0)
    ext[...] = jnp.zeros_like(ext)
    for u in range(GROUP):
        for side, place in ((0, 1), (0, 3), (1, 0), (1, 2)):
            ext[u, side, pl.ds(width + place, 1), :] = jnp.ones((1, TILE), jnp.float32)
    top[...] = jnp.full_like(top, FLOOR)
    total[...] = jnp.zeros_like(total)

    def extend(u, side, points, scale):
        square = jnp.sum(points * points, axis=0, keepdims=True) * SCALE
        high, middle = split(square)
        ext[u, side, pl.ds(0, width), :] = points * scale
        ext[u, side, pl.ds(width + side, 1), :] = square
        rest = square - high.astype(jnp.float32) - middle.astype(jnp.float32)
        ext[u, side, pl.ds(width + side + 2, 1), :] = rest
        return jnp.concatenate(split(ext[u, side]), axis=0)

    def group(q, carry):
        lax.fori_loop(q * GROUP, jnp.minimum(live, q * GROUP + GROUP), end, 0)
        ready = []
        for u in range(GROUP):
            k = q * GROUP + u
            centre = ys[k, :, pl.ds(0, 1)]
            left = extend(u, 0, xs[k] - centre, -2.0 * SCALE)
            right = extend(u, 1, ys[k] - centre, 1.0)
            lefts[k] = left
            rights[k] = right
            value = product(right, left)
            cost[k] = value
            peak = 0.0 - jnp.min(value, axis=0, keepdims=True)
            ready.append((k < live, block(tiles, 0, k, blocks_out), peak))
        for on, index, peak in ready:
            for h in range(2):
                new = jnp.where(on, peak[:, h * HALF : (h + 1) * HALF], FLOOR)
                top[row(index, h), :] = jnp.maximum(top[row(index, h), :], new)
        return carry

    lax.fori_loop(0, (live + GROUP - 1) // GROUP, group, 0)
    add_up(GROUP, live, tiles, 0, blocks_out, cost, lambda k: None, top, total)
    finish(out, top, total)


def turn_kernel(counts, lefts, rights, cost):
    live = counts[0, 0]

    def group(q, carry):
        for u in range(GROUP):
            k = q * GROUP + u
            cost[k] = product(lefts[k], rights[k])
        return carry

    lax.fori_loop(0, (live + GROUP - 1) // GROUP, group, 0)


def sweep_kernel(offset, far, last, inner, outer, blocks_in, blocks_out, tiles, counts, cost, *refs):
    parts = refs[:-6]
    out, result, held, top, total, rsem = refs[-6:]
    if far is None:
        top[...] = jnp.full_like(top, offset)
    else:
        top[...] = far - parts[0][...]
        parts = parts[1:]
    potential = offset - lse2_many([part[...] for part in parts])
    held[0] = potential
    if last:
        held[1] = potential / SCALE
        leave = pltpu.make_async_copy(held.at[1], result, rsem)
        leave.start()
    else:
        result[...] = potential
    total[...] = jnp.zeros_like(total)
    live = counts[0, 0]

    def potential_of(k):
        return spread(held, block(tiles, inner, k, blocks_in))

    least, most = add_up(WIDE, live, tiles, outer, blocks_out, cost, potential_of, top, total)
    finish(out, top, total)
    exact = (jnp.min(least) >= LEAST) & (jnp.max(most) <= MOST)

    @pl.when(jnp.logical_not(exact))
    def _():
        top[...] = jnp.full_like(top, FLOOR)
        total[...] = jnp.zeros_like(total)

        def step(k, carry):
            index = block(tiles, outer, k, blocks_out)
            found = peaks(k, cost, potential_of(k))
            for h in range(2):
                top[row(index, h), :] = jnp.maximum(top[row(index, h), :], found[h])
            return carry

        lax.fori_loop(0, live, step, 0)
        add_up(2, live, tiles, outer, blocks_out, cost, potential_of, top, total)
        finish(out, top, total)

    if last:
        leave.wait()


def vmem_spec():
    return pl.BlockSpec(memory_space=pltpu.VMEM)


def smem_spec():
    return pl.BlockSpec(memory_space=pltpu.SMEM)


def hbm_spec():
    return pl.BlockSpec(memory_space=pltpu.HBM)


def costs(tiles, counts, src, tgt, blocks_in, blocks_out):
    slots = tiles.shape[1]
    width = src.shape[0]
    part = pltpu.VMEM((slots, 2 * DEPTH, TILE), jnp.bfloat16)
    return pl.pallas_call(
        functools.partial(cost_kernel, blocks_in, blocks_out),
        out_shape=(
            pltpu.VMEM((slots, TILE, TILE), jnp.float32),
            jax.ShapeDtypeStruct((2 * blocks_out, HALF), jnp.float32),
            part,
            part,
            pltpu.SMEM(tiles.shape, jnp.int32),
        ),
        in_specs=[hbm_spec(), smem_spec(), hbm_spec(), hbm_spec()],
        out_specs=(vmem_spec(), vmem_spec(), vmem_spec(), vmem_spec(), smem_spec()),
        scratch_shapes=[
            pltpu.SemaphoreType.DMA(()),
            pltpu.VMEM((slots, width, TILE), jnp.float32),
            pltpu.VMEM((slots, width, TILE), jnp.float32),
            pltpu.VMEM((GROUP, 2, DEPTH, TILE), jnp.float32),
            pltpu.VMEM((2 * blocks_out, HALF), jnp.float32),
            pltpu.VMEM((2 * blocks_out, HALF), jnp.float32),
            pltpu.SemaphoreType.DMA((slots,)),
            pltpu.SemaphoreType.DMA((slots,)),
        ],
        compiler_params=pltpu.CompilerParams(vmem_limit_bytes=VMEM_LIMIT),
    )(tiles, counts, src, tgt)


def turned(counts, lefts, rights):
    slots = lefts.shape[0]
    return pl.pallas_call(
        turn_kernel,
        out_shape=pltpu.VMEM((slots, TILE, TILE), jnp.float32),
        in_specs=[smem_spec(), vmem_spec(), vmem_spec()],
        out_specs=vmem_spec(),
        compiler_params=pltpu.CompilerParams(vmem_limit_bytes=VMEM_LIMIT),
        cost_estimate=pl.CostEstimate(
            flops=slots * 8 * DEPTH * TILE * TILE, bytes_accessed=slots * 8 * TILE * TILE, transcendentals=0
        ),
    )(counts, lefts, rights)


def sweep(tiles, counts, cost, before, parts, cells, far_cells, inner, outer, blocks_in, blocks_out, last):
    far = None if before is None else math.log2(1.0 / far_cells)
    operands = list(parts) if before is None else [before, *parts]
    kernel = functools.partial(
        sweep_kernel, math.log2(1.0 / cells), far, last, inner, outer, blocks_in, blocks_out
    )
    return pl.pallas_call(
        kernel,
        out_shape=(
            jax.ShapeDtypeStruct((2 * blocks_out, HALF), jnp.float32),
            jax.ShapeDtypeStruct((2 * blocks_in, HALF), jnp.float32),
        ),
        in_specs=[smem_spec(), smem_spec()] + [vmem_spec()] * (1 + len(operands)),
        out_specs=(vmem_spec(), hbm_spec() if last else vmem_spec()),
        scratch_shapes=[
            pltpu.VMEM((2, 2 * blocks_in, HALF), jnp.float32),
            pltpu.VMEM((2 * blocks_out, HALF), jnp.float32),
            pltpu.VMEM((2 * blocks_out, HALF), jnp.float32),
            pltpu.SemaphoreType.DMA(()),
        ],
        compiler_params=pltpu.CompilerParams(vmem_limit_bytes=VMEM_LIMIT),
    )(tiles, counts, cost, *operands)


def swap(value, axis, flip):
    size = lax.axis_size(axis)
    return lax.ppermute(value, axis, [(k, k ^ flip) for k in range(size)])


def fan(value, axis, flips):
    total = value
    for flip in flips[:-1]:
        total = lax.optimization_barrier(lse2_many([total, swap(value, axis, flip)]))
    return lax.optimization_barrier([total, swap(value, axis, flips[-1])])


def over_core(value):
    return lse2_many([value, swap(value, "tgt", 1)])


def over_y(value):
    return fan(value, "tgt", (6, 4, 2))


def over_src(value):
    value = lse2_many([value, swap(value, "src", 28)])
    value = lax.optimization_barrier(lse2_many(fan(value, "src", (4, 12, 8))))
    return fan(value, "src", (3, 2, 1))


def body(src_points, tgt_points, tiles, counts):
    tiles, src_points, tgt_points = (
        pltpu.with_memory_space_constraint(each, pltpu.HBM)
        for each in (tiles[0, 0], src_points, tgt_points)
    )
    row_blocks = src_points.shape[1] // TILE
    col_blocks = tgt_points.shape[1] // TILE
    src_cells = src_points.shape[1] * lax.axis_size("src")
    tgt_cells = tgt_points.shape[1] * lax.axis_size("tgt")
    cost_ba, rows, lefts, rights, tiles = costs(
        tiles, counts, src_points, tgt_points, col_blocks, row_blocks
    )
    target = None
    for turn in range(ITERS):
        last = turn == ITERS - 1
        rows = over_core(rows)
        if turn == 0:
            rows, lefts = lax.optimization_barrier((rows, lefts))
            cost_ab = turned(counts, lefts, rights)
        cols, source = sweep(
            tiles, counts, cost_ab, target, over_y(rows), src_cells, tgt_cells, 0, 1,
            row_blocks, col_blocks, last,
        )
        parts = over_src(cols)
        if last:
            target = (math.log2(1.0 / tgt_cells) - lse2_many(parts)) / SCALE
        else:
            rows, target = sweep(
                tiles, counts, cost_ba, source, parts, tgt_cells, src_cells, 1, 0,
                col_blocks, row_blocks, False,
            )
    return (source.reshape(-1), target.reshape(-1))


def solution(mesh):
    in_specs = (P(None, "src"), P(None, "tgt"), P("src", "tgt", None, None), P("src", "tgt"))
    out_specs = (P("src"), P("tgt"))
    return jax.shard_map(body, mesh=mesh, in_specs=in_specs, out_specs=out_specs, check_vma=False)
```

```python
import functools
import math

import jax
import jax.numpy as jnp
from jax import lax
from jax.experimental import pallas as pl
from jax.experimental.pallas import tpu as pltpu
from jax.sharding import PartitionSpec as P

TILE = 256
HALF = 128
ROWS = 8
GROUP = 8
WIDE = 16
ITERS = 3
EPS = 0.05
FLOOR = -1e30
SCALE = 1.0 / (EPS * math.log(2.0))
DEPTH = 64
LEAST = 2.0**-80
MOST = 2.0**100
VMEM_LIMIT = 16 * 1024 * 1024


def lse2_many(parts):
    top = functools.reduce(jnp.maximum, parts)
    return top + jnp.log2(functools.reduce(jnp.add, [jnp.exp2(p - top) for p in parts]))


def split(value):
    high = value.astype(jnp.bfloat16)
    return high, (value - high.astype(jnp.float32)).astype(jnp.bfloat16)


def halves():
    return [(h, pl.ds(h * HALF, HALF)) for h in range(2)]


def row(index, h):
    return pl.ds(2 * index + h, 1)


def block(tiles, side, k, blocks):
    return jnp.minimum(tiles[side, k], blocks - 1)


def sums(k, cost, potential, shift):
    found = []
    for h, lanes in halves():
        kept = None
        for g, cells in halves():
            score = cost[k, cells, lanes]
            score = (0.0 - score if potential is None else potential[g] - score) - shift[h]
            part = jnp.sum(jnp.exp2(score).reshape(HALF // ROWS, ROWS, HALF), axis=0)
            kept = part if kept is None else kept + part
        found.append(jnp.sum(kept, axis=0, keepdims=True))
    return found


def peaks(k, cost, potential):
    found = []
    for h, lanes in halves():
        kept = None
        for g, cells in halves():
            score = cost[k, cells, lanes]
            score = 0.0 - score if potential is None else potential[g] - score
            part = jnp.max(score, axis=0, keepdims=True)
            kept = part if kept is None else jnp.maximum(kept, part)
        found.append(kept)
    return found


def spread(held, index):
    return [jnp.broadcast_to(held[0, row(index, g), :], (HALF, HALF)).T for g in range(2)]


def add_up(size, live, tiles, outer, blocks_out, cost, potential_of, top, total):
    def group(q, carry):
        least, most = carry
        ready = []
        for u in range(size):
            k = q * size + u
            out = block(tiles, outer, k, blocks_out)
            shift = [top[row(out, h), :] for h in range(2)]
            ready.append((k < live, out, sums(k, cost, potential_of(k), shift)))
        for on, out, found in ready:
            for h in range(2):
                total[row(out, h), :] = total[row(out, h), :] + jnp.where(on, found[h], 0.0)
                least = jnp.minimum(least, jnp.where(on, found[h], 1.0))
                most = jnp.maximum(most, jnp.where(on, found[h], 1.0))
        return least, most

    one = jnp.ones((1, HALF), jnp.float32)
    return lax.fori_loop(0, (live + size - 1) // size, group, (one, one))


def finish(out, top, total):
    found = total[...] > 0.0
    out[...] = jnp.where(found, top[...] + jnp.log2(jnp.where(found, total[...], 1.0)), FLOOR)


def product(first, second):
    turned = first.T
    turned = jnp.concatenate((turned, turned), axis=1)
    high, middle = second[:DEPTH], second[DEPTH:]
    other = jnp.concatenate((high, high, middle, middle), axis=0)
    return jnp.dot(turned, other, preferred_element_type=jnp.float32)


def cost_kernel(
    blocks_in, blocks_out, tiles_in, counts, src, tgt, cost, out, lefts, rights, tiles,
    tsem, xs, ys, ext, top, total, xsem, ysem
):
    table = pltpu.make_async_copy(tiles_in, tiles, tsem)
    table.start()
    table.wait()
    live = counts[0, 0]
    width = src.shape[0]

    def copies(k):
        first = pl.multiple_of(block(tiles, 0, k, blocks_out) * TILE, TILE)
        second = pl.multiple_of(block(tiles, 1, k, blocks_in) * TILE, TILE)
        return (
            pltpu.make_async_copy(src.at[:, pl.ds(first, TILE)], xs.at[k], xsem.at[k]),
            pltpu.make_async_copy(tgt.at[:, pl.ds(second, TILE)], ys.at[k], ysem.at[k]),
        )

    def begin(k, carry):
        for one in copies(k):
            one.start()
        return carry

    def end(k, carry):
        for one in copies(k):
            one.wait()
        return carry

    lax.fori_loop(0, live, begin, 0)
    ext[...] = jnp.zeros_like(ext)
    for u in range(GROUP):
        for side, place in ((0, 1), (0, 3), (1, 0), (1, 2)):
            ext[u, side, pl.ds(width + place, 1), :] = jnp.ones((1, TILE), jnp.float32)
    top[...] = jnp.full_like(top, FLOOR)
    total[...] = jnp.zeros_like(total)

    def extend(u, side, points, scale):
        square = jnp.sum(points * points, axis=0, keepdims=True) * SCALE
        high, middle = split(square)
        ext[u, side, pl.ds(0, width), :] = points * scale
        ext[u, side, pl.ds(width + side, 1), :] = square
        rest = square - high.astype(jnp.float32) - middle.astype(jnp.float32)
        ext[u, side, pl.ds(width + side + 2, 1), :] = rest
        return jnp.concatenate(split(ext[u, side]), axis=0)

    def group(q, carry):
        lax.fori_loop(q * GROUP, jnp.minimum(live, q * GROUP + GROUP), end, 0)
        ready = []
        for u in range(GROUP):
            k = q * GROUP + u
            centre = ys[k, :, pl.ds(0, 1)]
            left = extend(u, 0, xs[k] - centre, -2.0 * SCALE)
            right = extend(u, 1, ys[k] - centre, 1.0)
            lefts[k] = left
            rights[k] = right
            value = product(right, left)
            cost[k] = value
            peak = 0.0 - jnp.min(value, axis=0, keepdims=True)
            ready.append((k < live, block(tiles, 0, k, blocks_out), peak))
        for on, index, peak in ready:
            for h in range(2):
                new = jnp.where(on, peak[:, h * HALF : (h + 1) * HALF], FLOOR)
                top[row(index, h), :] = jnp.maximum(top[row(index, h), :], new)
        return carry

    lax.fori_loop(0, (live + GROUP - 1) // GROUP, group, 0)
    add_up(GROUP, live, tiles, 0, blocks_out, cost, lambda k: None, top, total)
    finish(out, top, total)


def turn_kernel(counts, lefts, rights, cost):
    live = counts[0, 0]

    def group(q, carry):
        for u in range(GROUP):
            k = q * GROUP + u
            cost[k] = product(lefts[k], rights[k])
        return carry

    lax.fori_loop(0, (live + GROUP - 1) // GROUP, group, 0)


def sweep_kernel(offset, far, last, inner, outer, blocks_in, blocks_out, tiles, counts, cost, *refs):
    parts = refs[:-6]
    out, result, held, top, total, rsem = refs[-6:]
    if far is None:
        top[...] = jnp.full_like(top, offset)
    else:
        top[...] = far - parts[0][...]
        parts = parts[1:]
    potential = offset - lse2_many([part[...] for part in parts])
    held[0] = potential
    if last:
        held[1] = potential / SCALE
        leave = pltpu.make_async_copy(held.at[1], result, rsem)
        leave.start()
    else:
        result[...] = potential
    total[...] = jnp.zeros_like(total)
    live = counts[0, 0]

    def potential_of(k):
        return spread(held, block(tiles, inner, k, blocks_in))

    least, most = add_up(WIDE, live, tiles, outer, blocks_out, cost, potential_of, top, total)
    finish(out, top, total)
    exact = (jnp.min(least) >= LEAST) & (jnp.max(most) <= MOST)

    @pl.when(jnp.logical_not(exact))
    def _():
        top[...] = jnp.full_like(top, FLOOR)
        total[...] = jnp.zeros_like(total)

        def step(k, carry):
            index = block(tiles, outer, k, blocks_out)
            found = peaks(k, cost, potential_of(k))
            for h in range(2):
                top[row(index, h), :] = jnp.maximum(top[row(index, h), :], found[h])
            return carry

        lax.fori_loop(0, live, step, 0)
        add_up(2, live, tiles, outer, blocks_out, cost, potential_of, top, total)
        finish(out, top, total)

    if last:
        leave.wait()


def vmem_spec():
    return pl.BlockSpec(memory_space=pltpu.VMEM)


def smem_spec():
    return pl.BlockSpec(memory_space=pltpu.SMEM)


def hbm_spec():
    return pl.BlockSpec(memory_space=pltpu.HBM)


def costs(tiles, counts, src, tgt, blocks_in, blocks_out):
    slots = tiles.shape[1]
    width = src.shape[0]
    part = pltpu.VMEM((slots, 2 * DEPTH, TILE), jnp.bfloat16)
    return pl.pallas_call(
        functools.partial(cost_kernel, blocks_in, blocks_out),
        out_shape=(
            pltpu.VMEM((slots, TILE, TILE), jnp.float32),
            jax.ShapeDtypeStruct((2 * blocks_out, HALF), jnp.float32),
            part,
            part,
            pltpu.SMEM(tiles.shape, jnp.int32),
        ),
        in_specs=[hbm_spec(), smem_spec(), hbm_spec(), hbm_spec()],
        out_specs=(vmem_spec(), vmem_spec(), vmem_spec(), vmem_spec(), smem_spec()),
        scratch_shapes=[
            pltpu.SemaphoreType.DMA(()),
            pltpu.VMEM((slots, width, TILE), jnp.float32),
            pltpu.VMEM((slots, width, TILE), jnp.float32),
            pltpu.VMEM((GROUP, 2, DEPTH, TILE), jnp.float32),
            pltpu.VMEM((2 * blocks_out, HALF), jnp.float32),
            pltpu.VMEM((2 * blocks_out, HALF), jnp.float32),
            pltpu.SemaphoreType.DMA((slots,)),
            pltpu.SemaphoreType.DMA((slots,)),
        ],
        compiler_params=pltpu.CompilerParams(vmem_limit_bytes=VMEM_LIMIT),
    )(tiles, counts, src, tgt)


def turned(counts, lefts, rights):
    slots = lefts.shape[0]
    return pl.pallas_call(
        turn_kernel,
        out_shape=pltpu.VMEM((slots, TILE, TILE), jnp.float32),
        in_specs=[smem_spec(), vmem_spec(), vmem_spec()],
        out_specs=vmem_spec(),
        compiler_params=pltpu.CompilerParams(vmem_limit_bytes=VMEM_LIMIT),
        cost_estimate=pl.CostEstimate(
            flops=slots * 8 * DEPTH * TILE * TILE, bytes_accessed=slots * 8 * TILE * TILE, transcendentals=0
        ),
    )(counts, lefts, rights)


def sweep(tiles, counts, cost, before, parts, cells, far_cells, inner, outer, blocks_in, blocks_out, last):
    far = None if before is None else math.log2(1.0 / far_cells)
    operands = list(parts) if before is None else [before, *parts]
    kernel = functools.partial(
        sweep_kernel, math.log2(1.0 / cells), far, last, inner, outer, blocks_in, blocks_out
    )
    return pl.pallas_call(
        kernel,
        out_shape=(
            jax.ShapeDtypeStruct((2 * blocks_out, HALF), jnp.float32),
            jax.ShapeDtypeStruct((2 * blocks_in, HALF), jnp.float32),
        ),
        in_specs=[smem_spec(), smem_spec()] + [vmem_spec()] * (1 + len(operands)),
        out_specs=(vmem_spec(), hbm_spec() if last else vmem_spec()),
        scratch_shapes=[
            pltpu.VMEM((2, 2 * blocks_in, HALF), jnp.float32),
            pltpu.VMEM((2 * blocks_out, HALF), jnp.float32),
            pltpu.VMEM((2 * blocks_out, HALF), jnp.float32),
            pltpu.SemaphoreType.DMA(()),
        ],
        compiler_params=pltpu.CompilerParams(vmem_limit_bytes=VMEM_LIMIT),
    )(tiles, counts, cost, *operands)


def swap(value, axis, flip):
    size = lax.axis_size(axis)
    return lax.ppermute(value, axis, [(k, k ^ flip) for k in range(size)])


def fan(value, axis, flips):
    return [value, *[swap(value, axis, flip) for flip in flips]]


def over_core(value):
    return lse2_many(fan(value, "tgt", (1,)))


def over_y(value):
    return fan(value, "tgt", (6, 4, 2))


def over_src(value):
    value = lse2_many(fan(value, "src", (3, 2, 1)))
    value = lse2_many(fan(value, "src", (4,)))
    value = lse2_many(fan(value, "src", (12,)))
    return fan(value, "src", (28,))


def body(src_points, tgt_points, tiles, counts):
    tiles, src_points, tgt_points = (
        pltpu.with_memory_space_constraint(each, pltpu.HBM)
        for each in (tiles[0, 0], src_points, tgt_points)
    )
    row_blocks = src_points.shape[1] // TILE
    col_blocks = tgt_points.shape[1] // TILE
    src_cells = src_points.shape[1] * lax.axis_size("src")
    tgt_cells = tgt_points.shape[1] * lax.axis_size("tgt")
    cost_ba, rows, lefts, rights, tiles = costs(
        tiles, counts, src_points, tgt_points, col_blocks, row_blocks
    )
    target = None
    for turn in range(ITERS):
        last = turn == ITERS - 1
        rows = over_core(rows)
        if turn == 0:
            rows, lefts = lax.optimization_barrier((rows, lefts))
            cost_ab = turned(counts, lefts, rights)
        cols, source = sweep(
            tiles, counts, cost_ab, target, over_y(rows), src_cells, tgt_cells, 0, 1,
            row_blocks, col_blocks, last,
        )
        parts = over_src(cols)
        if last:
            target = (math.log2(1.0 / tgt_cells) - lse2_many(parts)) / SCALE
        else:
            rows, target = sweep(
                tiles, counts, cost_ba, source, parts, tgt_cells, src_cells, 1, 0,
                col_blocks, row_blocks, False,
            )
    return (source.reshape(-1), target.reshape(-1))


def solution(mesh):
    in_specs = (P(None, "src"), P(None, "tgt"), P("src", "tgt", None, None), P("src", "tgt"))
    out_specs = (P("src"), P("tgt"))
    return jax.shard_map(body, mesh=mesh, in_specs=in_specs, out_specs=out_specs, check_vma=False)
```

```python
import functools
import math

import jax
import jax.numpy as jnp
from jax import lax
from jax.experimental import pallas as pl
from jax.experimental.pallas import tpu as pltpu
from jax.sharding import PartitionSpec as P

TILE = 256
HALF = 128
ROWS = 8
GROUP = 8
WIDE = 16
ITERS = 3
EPS = 0.05
FLOOR = -1e30
SCALE = 1.0 / (EPS * math.log(2.0))
DEPTH = 64
LEAST = 2.0**-80
MOST = 2.0**100
VMEM_LIMIT = 16 * 1024 * 1024


def lse2_many(parts):
    top = functools.reduce(jnp.maximum, parts)
    return top + jnp.log2(functools.reduce(jnp.add, [jnp.exp2(p - top) for p in parts]))


def split(value):
    high = value.astype(jnp.bfloat16)
    return high, (value - high.astype(jnp.float32)).astype(jnp.bfloat16)


def halves():
    return [(h, pl.ds(h * HALF, HALF)) for h in range(2)]


def row(index, h):
    return pl.ds(2 * index + h, 1)


def block(tiles, side, k, blocks):
    return jnp.minimum(tiles[side, k], blocks - 1)


def sums(k, cost, potential, shift):
    found = []
    for h, lanes in halves():
        kept = None
        for g, cells in halves():
            score = cost[k, cells, lanes]
            score = (0.0 - score if potential is None else potential[g] - score) - shift[h]
            part = jnp.sum(jnp.exp2(score).reshape(HALF // ROWS, ROWS, HALF), axis=0)
            kept = part if kept is None else kept + part
        found.append(jnp.sum(kept, axis=0, keepdims=True))
    return found


def peaks(k, cost, potential):
    found = []
    for h, lanes in halves():
        kept = None
        for g, cells in halves():
            score = cost[k, cells, lanes]
            score = 0.0 - score if potential is None else potential[g] - score
            part = jnp.max(score, axis=0, keepdims=True)
            kept = part if kept is None else jnp.maximum(kept, part)
        found.append(kept)
    return found


def spread(held, index):
    return [jnp.broadcast_to(held[0, row(index, g), :], (HALF, HALF)).T for g in range(2)]


def add_up(size, live, tiles, outer, blocks_out, cost, potential_of, top, total):
    def group(q, carry):
        least, most = carry
        ready = []
        for u in range(size):
            k = q * size + u
            out = block(tiles, outer, k, blocks_out)
            shift = [top[row(out, h), :] for h in range(2)]
            ready.append((k < live, out, sums(k, cost, potential_of(k), shift)))
        for on, out, found in ready:
            for h in range(2):
                total[row(out, h), :] = total[row(out, h), :] + jnp.where(on, found[h], 0.0)
                least = jnp.minimum(least, jnp.where(on, found[h], 1.0))
                most = jnp.maximum(most, jnp.where(on, found[h], 1.0))
        return least, most

    one = jnp.ones((1, HALF), jnp.float32)
    return lax.fori_loop(0, (live + size - 1) // size, group, (one, one))


def finish(out, top, total):
    found = total[...] > 0.0
    out[...] = jnp.where(found, top[...] + jnp.log2(jnp.where(found, total[...], 1.0)), FLOOR)


def product(first, second):
    turned = first.T
    turned = jnp.concatenate((turned, turned), axis=1)
    high, middle = second[:DEPTH], second[DEPTH:]
    other = jnp.concatenate((high, high, middle, middle), axis=0)
    return jnp.dot(turned, other, preferred_element_type=jnp.float32)


def cost_kernel(
    blocks_in, blocks_out, tiles_in, counts, src, tgt, cost, out, lefts, rights, tiles,
    tsem, xs, ys, ext, top, total, xsem, ysem
):
    table = pltpu.make_async_copy(tiles_in, tiles, tsem)
    table.start()
    width = src.shape[0]
    ext[...] = jnp.zeros_like(ext)
    for u in range(GROUP):
        for side, place in ((0, 1), (0, 3), (1, 0), (1, 2)):
            ext[u, side, pl.ds(width + place, 1), :] = jnp.ones((1, TILE), jnp.float32)
    top[...] = jnp.full_like(top, FLOOR)
    total[...] = jnp.zeros_like(total)
    table.wait()
    live = counts[0, 0]

    def copies(k):
        first = pl.multiple_of(block(tiles, 0, k, blocks_out) * TILE, TILE)
        second = pl.multiple_of(block(tiles, 1, k, blocks_in) * TILE, TILE)
        return (
            pltpu.make_async_copy(src.at[:, pl.ds(first, TILE)], xs.at[k], xsem.at[k]),
            pltpu.make_async_copy(tgt.at[:, pl.ds(second, TILE)], ys.at[k], ysem.at[k]),
        )

    def begin(k, carry):
        for one in copies(k):
            one.start()
        return carry

    def end(k, carry):
        for one in copies(k):
            one.wait()
        return carry

    lax.fori_loop(0, live, begin, 0)

    def extend(u, side, points, scale):
        square = jnp.sum(points * points, axis=0, keepdims=True) * SCALE
        high, middle = split(square)
        ext[u, side, pl.ds(0, width), :] = points * scale
        ext[u, side, pl.ds(width + side, 1), :] = square
        rest = square - high.astype(jnp.float32) - middle.astype(jnp.float32)
        ext[u, side, pl.ds(width + side + 2, 1), :] = rest
        return jnp.concatenate(split(ext[u, side]), axis=0)

    def group(q, carry):
        lax.fori_loop(q * GROUP, jnp.minimum(live, q * GROUP + GROUP), end, 0)
        ready = []
        for u in range(GROUP):
            k = q * GROUP + u
            centre = ys[k, :, pl.ds(0, 1)]
            left = extend(u, 0, xs[k] - centre, -2.0 * SCALE)
            right = extend(u, 1, ys[k] - centre, 1.0)
            lefts[k] = left
            rights[k] = right
            value = product(right, left)
            cost[k] = value
            peak = 0.0 - jnp.min(value, axis=0, keepdims=True)
            ready.append((k < live, block(tiles, 0, k, blocks_out), peak))
        for on, index, peak in ready:
            for h in range(2):
                new = jnp.where(on, peak[:, h * HALF : (h + 1) * HALF], FLOOR)
                top[row(index, h), :] = jnp.maximum(top[row(index, h), :], new)
        return carry

    lax.fori_loop(0, (live + GROUP - 1) // GROUP, group, 0)
    add_up(WIDE, live, tiles, 0, blocks_out, cost, lambda k: None, top, total)
    finish(out, top, total)


def turn_kernel(counts, lefts, rights, cost):
    live = counts[0, 0]

    def group(q, carry):
        for u in range(GROUP):
            k = q * GROUP + u
            cost[k] = product(lefts[k], rights[k])
        return carry

    lax.fori_loop(0, (live + GROUP - 1) // GROUP, group, 0)


def sweep_kernel(offset, far, last, inner, outer, blocks_in, blocks_out, tiles, counts, cost, *refs):
    parts = refs[:-6]
    out, result, held, top, total, rsem = refs[-6:]
    if far is None:
        top[...] = jnp.full_like(top, offset)
    else:
        top[...] = far - parts[0][...]
        parts = parts[1:]
    potential = offset - lse2_many([part[...] for part in parts])
    held[0] = potential
    if last:
        held[1] = potential / SCALE
        leave = pltpu.make_async_copy(held.at[1], result, rsem)
        leave.start()
    else:
        result[...] = potential
    total[...] = jnp.zeros_like(total)
    live = counts[0, 0]

    def potential_of(k):
        return spread(held, block(tiles, inner, k, blocks_in))

    least, most = add_up(WIDE, live, tiles, outer, blocks_out, cost, potential_of, top, total)
    finish(out, top, total)
    exact = (jnp.min(least) >= LEAST) & (jnp.max(most) <= MOST)

    @pl.when(jnp.logical_not(exact))
    def _():
        top[...] = jnp.full_like(top, FLOOR)
        total[...] = jnp.zeros_like(total)

        def step(k, carry):
            index = block(tiles, outer, k, blocks_out)
            found = peaks(k, cost, potential_of(k))
            for h in range(2):
                top[row(index, h), :] = jnp.maximum(top[row(index, h), :], found[h])
            return carry

        lax.fori_loop(0, live, step, 0)
        add_up(2, live, tiles, outer, blocks_out, cost, potential_of, top, total)
        finish(out, top, total)

    if last:
        leave.wait()


def vmem_spec():
    return pl.BlockSpec(memory_space=pltpu.VMEM)


def smem_spec():
    return pl.BlockSpec(memory_space=pltpu.SMEM)


def hbm_spec():
    return pl.BlockSpec(memory_space=pltpu.HBM)


def costs(tiles, counts, src, tgt, blocks_in, blocks_out):
    slots = tiles.shape[1]
    width = src.shape[0]
    part = pltpu.VMEM((slots, 2 * DEPTH, TILE), jnp.bfloat16)
    return pl.pallas_call(
        functools.partial(cost_kernel, blocks_in, blocks_out),
        out_shape=(
            pltpu.VMEM((slots, TILE, TILE), jnp.float32),
            jax.ShapeDtypeStruct((2 * blocks_out, HALF), jnp.float32),
            part,
            part,
            pltpu.SMEM(tiles.shape, jnp.int32),
        ),
        in_specs=[hbm_spec(), smem_spec(), hbm_spec(), hbm_spec()],
        out_specs=(vmem_spec(), vmem_spec(), vmem_spec(), vmem_spec(), smem_spec()),
        scratch_shapes=[
            pltpu.SemaphoreType.DMA(()),
            pltpu.VMEM((slots, width, TILE), jnp.float32),
            pltpu.VMEM((slots, width, TILE), jnp.float32),
            pltpu.VMEM((GROUP, 2, DEPTH, TILE), jnp.float32),
            pltpu.VMEM((2 * blocks_out, HALF), jnp.float32),
            pltpu.VMEM((2 * blocks_out, HALF), jnp.float32),
            pltpu.SemaphoreType.DMA((slots,)),
            pltpu.SemaphoreType.DMA((slots,)),
        ],
        compiler_params=pltpu.CompilerParams(vmem_limit_bytes=VMEM_LIMIT),
    )(tiles, counts, src, tgt)


def turned(counts, lefts, rights):
    slots = lefts.shape[0]
    return pl.pallas_call(
        turn_kernel,
        out_shape=pltpu.VMEM((slots, TILE, TILE), jnp.float32),
        in_specs=[smem_spec(), vmem_spec(), vmem_spec()],
        out_specs=vmem_spec(),
        compiler_params=pltpu.CompilerParams(vmem_limit_bytes=VMEM_LIMIT),
        cost_estimate=pl.CostEstimate(
            flops=slots * 8 * DEPTH * TILE * TILE, bytes_accessed=slots * 8 * TILE * TILE, transcendentals=0
        ),
    )(counts, lefts, rights)


def sweep(tiles, counts, cost, before, parts, cells, far_cells, inner, outer, blocks_in, blocks_out, last):
    far = None if before is None else math.log2(1.0 / far_cells)
    operands = list(parts) if before is None else [before, *parts]
    kernel = functools.partial(
        sweep_kernel, math.log2(1.0 / cells), far, last, inner, outer, blocks_in, blocks_out
    )
    return pl.pallas_call(
        kernel,
        out_shape=(
            jax.ShapeDtypeStruct((2 * blocks_out, HALF), jnp.float32),
            jax.ShapeDtypeStruct((2 * blocks_in, HALF), jnp.float32),
        ),
        in_specs=[smem_spec(), smem_spec()] + [vmem_spec()] * (1 + len(operands)),
        out_specs=(vmem_spec(), hbm_spec() if last else vmem_spec()),
        scratch_shapes=[
            pltpu.VMEM((2, 2 * blocks_in, HALF), jnp.float32),
            pltpu.VMEM((2 * blocks_out, HALF), jnp.float32),
            pltpu.VMEM((2 * blocks_out, HALF), jnp.float32),
            pltpu.SemaphoreType.DMA(()),
        ],
        compiler_params=pltpu.CompilerParams(vmem_limit_bytes=VMEM_LIMIT),
    )(tiles, counts, cost, *operands)


def swap(value, axis, flip):
    size = lax.axis_size(axis)
    return lax.ppermute(value, axis, [(k, k ^ flip) for k in range(size)])


def fan(value, axis, flips):
    return [value, *[swap(value, axis, flip) for flip in flips]]


def over_core(value):
    return lse2_many(fan(value, "tgt", (1,)))


def over_y(value):
    return fan(value, "tgt", (6, 4, 2))


def over_src(value):
    for flip in (28, 12, 4):
        value = lse2_many(fan(value, "src", (flip,)))
    return fan(value, "src", (3, 2, 1))


def body(src_points, tgt_points, tiles, counts):
    tiles, src_points, tgt_points = (
        pltpu.with_memory_space_constraint(each, pltpu.HBM)
        for each in (tiles[0, 0], src_points, tgt_points)
    )
    row_blocks = src_points.shape[1] // TILE
    col_blocks = tgt_points.shape[1] // TILE
    src_cells = src_points.shape[1] * lax.axis_size("src")
    tgt_cells = tgt_points.shape[1] * lax.axis_size("tgt")
    cost_ba, rows, lefts, rights, tiles = costs(
        tiles, counts, src_points, tgt_points, col_blocks, row_blocks
    )
    target = None
    for turn in range(ITERS):
        last = turn == ITERS - 1
        rows = over_core(rows)
        if turn == 0:
            rows, lefts = lax.optimization_barrier((rows, lefts))
            cost_ab = turned(counts, lefts, rights)
        cols, source = sweep(
            tiles, counts, cost_ab, target, over_y(rows), src_cells, tgt_cells, 0, 1,
            row_blocks, col_blocks, last,
        )
        parts = over_src(cols)
        if last:
            target = (math.log2(1.0 / tgt_cells) - lse2_many(parts)) / SCALE
        else:
            rows, target = sweep(
                tiles, counts, cost_ba, source, parts, tgt_cells, src_cells, 1, 0,
                col_blocks, row_blocks, False,
            )
    return (source.reshape(-1), target.reshape(-1))


def solution(mesh):
    in_specs = (P(None, "src"), P(None, "tgt"), P("src", "tgt", None, None), P("src", "tgt"))
    out_specs = (P("src"), P("tgt"))
    return jax.shard_map(body, mesh=mesh, in_specs=in_specs, out_specs=out_specs, check_vma=False)
```

```python
import functools
import math

import jax
import jax.numpy as jnp
from jax import lax
from jax.experimental import pallas as pl
from jax.experimental.pallas import tpu as pltpu
from jax.sharding import PartitionSpec as P

TILE = 256
HALF = 128
ROWS = 8
GROUP = 8
WIDE = 16
ITERS = 3
EPS = 0.05
FLOOR = -1e30
SCALE = 1.0 / (EPS * math.log(2.0))
DEPTH = 64
LEAST = 2.0**-80
MOST = 2.0**100
VMEM_LIMIT = 16 * 1024 * 1024


def lse2_many(parts):
    top = functools.reduce(jnp.maximum, parts)
    return top + jnp.log2(functools.reduce(jnp.add, [jnp.exp2(p - top) for p in parts]))


def split(value):
    high = value.astype(jnp.bfloat16)
    return high, (value - high.astype(jnp.float32)).astype(jnp.bfloat16)


def halves():
    return [(h, pl.ds(h * HALF, HALF)) for h in range(2)]


def row(index, h):
    return pl.ds(2 * index + h, 1)


def block(tiles, side, k, blocks):
    return jnp.minimum(tiles[side, k], blocks - 1)


def sums(k, cost, potential, shift):
    found = []
    for h, lanes in halves():
        kept = None
        for g, cells in halves():
            score = cost[k, cells, lanes]
            score = (0.0 - score if potential is None else potential[g] - score) - shift[h]
            part = jnp.sum(jnp.exp2(score).reshape(HALF // ROWS, ROWS, HALF), axis=0)
            kept = part if kept is None else kept + part
        found.append(jnp.sum(kept, axis=0, keepdims=True))
    return found


def peaks(k, cost, potential):
    found = []
    for h, lanes in halves():
        kept = None
        for g, cells in halves():
            score = cost[k, cells, lanes]
            score = 0.0 - score if potential is None else potential[g] - score
            part = jnp.max(score, axis=0, keepdims=True)
            kept = part if kept is None else jnp.maximum(kept, part)
        found.append(kept)
    return found


def spread(held, index):
    return [jnp.broadcast_to(held[0, row(index, g), :], (HALF, HALF)).T for g in range(2)]


def add_up(size, live, tiles, outer, blocks_out, cost, potential_of, top, total):
    def group(q, carry):
        least, most = carry
        ready = []
        for u in range(size):
            k = q * size + u
            out = block(tiles, outer, k, blocks_out)
            shift = [top[row(out, h), :] for h in range(2)]
            ready.append((k < live, out, sums(k, cost, potential_of(k), shift)))
        for on, out, found in ready:
            for h in range(2):
                total[row(out, h), :] = total[row(out, h), :] + jnp.where(on, found[h], 0.0)
                least = jnp.minimum(least, jnp.where(on, found[h], 1.0))
                most = jnp.maximum(most, jnp.where(on, found[h], 1.0))
        return least, most

    one = jnp.ones((1, HALF), jnp.float32)
    return lax.fori_loop(0, (live + size - 1) // size, group, (one, one))


def finish(out, top, total):
    found = total[...] > 0.0
    out[...] = jnp.where(found, top[...] + jnp.log2(jnp.where(found, total[...], 1.0)), FLOOR)


def product(first, second):
    turned = first.T
    turned = jnp.concatenate((turned, turned), axis=1)
    high, middle = second[:DEPTH], second[DEPTH:]
    other = jnp.concatenate((high, high, middle, middle), axis=0)
    return jnp.dot(turned, other, preferred_element_type=jnp.float32)


def cost_kernel(
    blocks_in, blocks_out, tiles_in, counts, src, tgt, cost, out, lefts, rights, tiles,
    tsem, xs, ys, ext, top, total, xsem, ysem
):
    table = pltpu.make_async_copy(tiles_in, tiles, tsem)
    table.start()
    width = src.shape[0]
    ext[...] = jnp.zeros_like(ext)
    for u in range(GROUP):
        for side, place in ((0, 1), (0, 3), (1, 0), (1, 2)):
            ext[u, side, pl.ds(width + place, 1), :] = jnp.ones((1, TILE), jnp.float32)
    top[...] = jnp.full_like(top, FLOOR)
    total[...] = jnp.zeros_like(total)
    table.wait()
    live = counts[0, 0]

    def copies(k):
        first = pl.multiple_of(block(tiles, 0, k, blocks_out) * TILE, TILE)
        second = pl.multiple_of(block(tiles, 1, k, blocks_in) * TILE, TILE)
        return (
            pltpu.make_async_copy(src.at[:, pl.ds(first, TILE)], xs.at[k], xsem.at[k]),
            pltpu.make_async_copy(tgt.at[:, pl.ds(second, TILE)], ys.at[k], ysem.at[k]),
        )

    def begin(k, carry):
        for one in copies(k):
            one.start()
        return carry

    def end(k, carry):
        for one in copies(k):
            one.wait()
        return carry

    lax.fori_loop(0, live, begin, 0)

    def extend(u, side, points, scale):
        square = jnp.sum(points * points, axis=0, keepdims=True) * SCALE
        high, middle = split(square)
        ext[u, side, pl.ds(0, width), :] = points * scale
        ext[u, side, pl.ds(width + side, 1), :] = square
        rest = square - high.astype(jnp.float32) - middle.astype(jnp.float32)
        ext[u, side, pl.ds(width + side + 2, 1), :] = rest
        return jnp.concatenate(split(ext[u, side]), axis=0)

    def group(q, carry):
        lax.fori_loop(q * GROUP, jnp.minimum(live, q * GROUP + GROUP), end, 0)
        ready = []
        for u in range(GROUP):
            k = q * GROUP + u
            centre = ys[k, :, pl.ds(0, 1)]
            left = extend(u, 0, xs[k] - centre, -2.0 * SCALE)
            right = extend(u, 1, ys[k] - centre, 1.0)
            lefts[k] = left
            rights[k] = right
            value = product(right, left)
            cost[k] = value
            peak = 0.0 - jnp.min(value, axis=0, keepdims=True)
            ready.append((k < live, block(tiles, 0, k, blocks_out), peak))
        for on, index, peak in ready:
            for h in range(2):
                new = jnp.where(on, peak[:, h * HALF : (h + 1) * HALF], FLOOR)
                top[row(index, h), :] = jnp.maximum(top[row(index, h), :], new)
        return carry

    lax.fori_loop(0, (live + GROUP - 1) // GROUP, group, 0)
    add_up(WIDE, live, tiles, 0, blocks_out, cost, lambda k: None, top, total)
    finish(out, top, total)


def turn_kernel(counts, lefts, rights, cost):
    live = counts[0, 0]

    def group(q, carry):
        for u in range(GROUP):
            k = q * GROUP + u
            cost[k] = product(lefts[k], rights[k])
        return carry

    lax.fori_loop(0, (live + GROUP - 1) // GROUP, group, 0)


def sweep_kernel(offset, far, last, inner, outer, blocks_in, blocks_out, tiles, counts, cost, *refs):
    parts = refs[:-6]
    out, result, held, top, total, rsem = refs[-6:]
    if far is None:
        top[...] = jnp.full_like(top, offset)
    else:
        top[...] = far - parts[0][...]
        parts = parts[1:]
    potential = offset - lse2_many([part[...] for part in parts])
    held[0] = potential
    if last:
        held[1] = potential / SCALE
        leave = pltpu.make_async_copy(held.at[1], result, rsem)
        leave.start()
    else:
        result[...] = potential
    total[...] = jnp.zeros_like(total)
    live = counts[0, 0]

    def potential_of(k):
        return spread(held, block(tiles, inner, k, blocks_in))

    least, most = add_up(WIDE, live, tiles, outer, blocks_out, cost, potential_of, top, total)
    finish(out, top, total)
    exact = (jnp.min(least) >= LEAST) & (jnp.max(most) <= MOST)

    @pl.when(jnp.logical_not(exact))
    def _():
        top[...] = jnp.full_like(top, FLOOR)
        total[...] = jnp.zeros_like(total)

        def step(k, carry):
            index = block(tiles, outer, k, blocks_out)
            found = peaks(k, cost, potential_of(k))
            for h in range(2):
                top[row(index, h), :] = jnp.maximum(top[row(index, h), :], found[h])
            return carry

        lax.fori_loop(0, live, step, 0)
        add_up(2, live, tiles, outer, blocks_out, cost, potential_of, top, total)
        finish(out, top, total)

    if last:
        leave.wait()


def vmem_spec():
    return pl.BlockSpec(memory_space=pltpu.VMEM)


def smem_spec():
    return pl.BlockSpec(memory_space=pltpu.SMEM)


def hbm_spec():
    return pl.BlockSpec(memory_space=pltpu.HBM)


def costs(tiles, counts, src, tgt, blocks_in, blocks_out):
    slots = tiles.shape[1]
    width = src.shape[0]
    part = pltpu.VMEM((slots, 2 * DEPTH, TILE), jnp.bfloat16)
    return pl.pallas_call(
        functools.partial(cost_kernel, blocks_in, blocks_out),
        out_shape=(
            pltpu.VMEM((slots, TILE, TILE), jnp.float32),
            jax.ShapeDtypeStruct((2 * blocks_out, HALF), jnp.float32),
            part,
            part,
            pltpu.SMEM(tiles.shape, jnp.int32),
        ),
        in_specs=[hbm_spec(), smem_spec(), hbm_spec(), hbm_spec()],
        out_specs=(vmem_spec(), vmem_spec(), vmem_spec(), vmem_spec(), smem_spec()),
        scratch_shapes=[
            pltpu.SemaphoreType.DMA(()),
            pltpu.VMEM((slots, width, TILE), jnp.float32),
            pltpu.VMEM((slots, width, TILE), jnp.float32),
            pltpu.VMEM((GROUP, 2, DEPTH, TILE), jnp.float32),
            pltpu.VMEM((2 * blocks_out, HALF), jnp.float32),
            pltpu.VMEM((2 * blocks_out, HALF), jnp.float32),
            pltpu.SemaphoreType.DMA((slots,)),
            pltpu.SemaphoreType.DMA((slots,)),
        ],
        compiler_params=pltpu.CompilerParams(vmem_limit_bytes=VMEM_LIMIT),
    )(tiles, counts, src, tgt)


def turned(counts, lefts, rights):
    slots = lefts.shape[0]
    return pl.pallas_call(
        turn_kernel,
        out_shape=pltpu.VMEM((slots, TILE, TILE), jnp.float32),
        in_specs=[smem_spec(), vmem_spec(), vmem_spec()],
        out_specs=vmem_spec(),
        compiler_params=pltpu.CompilerParams(vmem_limit_bytes=VMEM_LIMIT),
        cost_estimate=pl.CostEstimate(
            flops=slots * 8 * DEPTH * TILE * TILE, bytes_accessed=slots * 8 * TILE * TILE, transcendentals=0
        ),
    )(counts, lefts, rights)


def sweep(tiles, counts, cost, before, parts, cells, far_cells, inner, outer, blocks_in, blocks_out, last):
    far = None if before is None else math.log2(1.0 / far_cells)
    operands = list(parts) if before is None else [before, *parts]
    kernel = functools.partial(
        sweep_kernel, math.log2(1.0 / cells), far, last, inner, outer, blocks_in, blocks_out
    )
    return pl.pallas_call(
        kernel,
        out_shape=(
            jax.ShapeDtypeStruct((2 * blocks_out, HALF), jnp.float32),
            jax.ShapeDtypeStruct((2 * blocks_in, HALF), jnp.float32),
        ),
        in_specs=[smem_spec(), smem_spec()] + [vmem_spec()] * (1 + len(operands)),
        out_specs=(vmem_spec(), hbm_spec() if last else vmem_spec()),
        scratch_shapes=[
            pltpu.VMEM((2, 2 * blocks_in, HALF), jnp.float32),
            pltpu.VMEM((2 * blocks_out, HALF), jnp.float32),
            pltpu.VMEM((2 * blocks_out, HALF), jnp.float32),
            pltpu.SemaphoreType.DMA(()),
        ],
        compiler_params=pltpu.CompilerParams(vmem_limit_bytes=VMEM_LIMIT),
    )(tiles, counts, cost, *operands)


def swap(value, axis, flips):
    src, tgt = lax.axis_size("src"), lax.axis_size("tgt")
    pairs = []
    for s in range(src):
        for t in range(tgt):
            flip = flips[t % 2]
            other = (s ^ flip, t) if axis == "src" else (s, t ^ flip)
            pairs.append((s * tgt + t, other[0] * tgt + other[1]))
    return lax.ppermute(value, ("src", "tgt"), pairs)


def fan(value, axis, *flips):
    return [value, *[swap(value, axis, each) for each in flips]]


def over_core(value):
    return lse2_many(fan(value, "tgt", (1, 1)))


def over_y(value):
    return fan(value, "tgt", (6, 4), (4, 6), (2, 2))


def over_src(value):
    for flips in ((28, 12), (12, 28), (4, 4)):
        value = lse2_many(fan(value, "src", flips))
    return fan(value, "src", (3, 2), (2, 3), (1, 1))


def body(src_points, tgt_points, tiles, counts):
    tiles, src_points, tgt_points = (
        pltpu.with_memory_space_constraint(each, pltpu.HBM)
        for each in (tiles[0, 0], src_points, tgt_points)
    )
    row_blocks = src_points.shape[1] // TILE
    col_blocks = tgt_points.shape[1] // TILE
    src_cells = src_points.shape[1] * lax.axis_size("src")
    tgt_cells = tgt_points.shape[1] * lax.axis_size("tgt")
    cost_ba, rows, lefts, rights, tiles = costs(
        tiles, counts, src_points, tgt_points, col_blocks, row_blocks
    )
    target = None
    for turn in range(ITERS):
        last = turn == ITERS - 1
        rows = over_core(rows)
        if turn == 0:
            rows, lefts = lax.optimization_barrier((rows, lefts))
            cost_ab = turned(counts, lefts, rights)
        cols, source = sweep(
            tiles, counts, cost_ab, target, over_y(rows), src_cells, tgt_cells, 0, 1,
            row_blocks, col_blocks, last,
        )
        parts = over_src(cols)
        if last:
            target = (math.log2(1.0 / tgt_cells) - lse2_many(parts)) / SCALE
        else:
            rows, target = sweep(
                tiles, counts, cost_ba, source, parts, tgt_cells, src_cells, 1, 0,
                col_blocks, row_blocks, False,
            )
    return (source.reshape(-1), target.reshape(-1))


def solution(mesh):
    in_specs = (P(None, "src"), P(None, "tgt"), P("src", "tgt", None, None), P("src", "tgt"))
    out_specs = (P("src"), P("tgt"))
    return jax.shard_map(body, mesh=mesh, in_specs=in_specs, out_specs=out_specs, check_vma=False)
```

```python
import functools
import math

import jax
import jax.numpy as jnp
from jax import lax
from jax.experimental import pallas as pl
from jax.experimental.pallas import tpu as pltpu
from jax.sharding import PartitionSpec as P

TILE = 256
HALF = 128
ROWS = 8
GROUP = 8
WIDE = 16
ITERS = 3
EPS = 0.05
FLOOR = -1e30
SCALE = 1.0 / (EPS * math.log(2.0))
DEPTH = 64
LEAST = 2.0**-80
MOST = 2.0**100
VMEM_LIMIT = 16 * 1024 * 1024


def lse2_many(parts):
    top = functools.reduce(jnp.maximum, parts)
    return top + jnp.log2(functools.reduce(jnp.add, [jnp.exp2(p - top) for p in parts]))


def split(value):
    high = value.astype(jnp.bfloat16)
    return high, (value - high.astype(jnp.float32)).astype(jnp.bfloat16)


def halves():
    return [(h, pl.ds(h * HALF, HALF)) for h in range(2)]


def row(index, h):
    return pl.ds(2 * index + h, 1)


def block(tiles, side, k, blocks):
    return jnp.minimum(tiles[side, k], blocks - 1)


def sums(k, cost, potential, shift):
    found = []
    for h, lanes in halves():
        kept = None
        for g, cells in halves():
            score = cost[k, cells, lanes]
            score = (0.0 - score if potential is None else potential[g] - score) - shift[h]
            part = jnp.sum(jnp.exp2(score).reshape(HALF // ROWS, ROWS, HALF), axis=0)
            kept = part if kept is None else kept + part
        found.append(jnp.sum(kept, axis=0, keepdims=True))
    return found


def peaks(k, cost, potential):
    found = []
    for h, lanes in halves():
        kept = None
        for g, cells in halves():
            score = cost[k, cells, lanes]
            score = 0.0 - score if potential is None else potential[g] - score
            part = jnp.max(score, axis=0, keepdims=True)
            kept = part if kept is None else jnp.maximum(kept, part)
        found.append(kept)
    return found


def spread(held, index):
    return [jnp.broadcast_to(held[0, row(index, g), :], (HALF, HALF)).T for g in range(2)]


def add_up(size, live, tiles, outer, blocks_out, cost, potential_of, top, total):
    def group(q, carry):
        least, most = carry
        ready = []
        for u in range(size):
            k = q * size + u
            out = block(tiles, outer, k, blocks_out)
            shift = [top[row(out, h), :] for h in range(2)]
            ready.append((k < live, out, sums(k, cost, potential_of(k), shift)))
        for on, out, found in ready:
            for h in range(2):
                total[row(out, h), :] = total[row(out, h), :] + jnp.where(on, found[h], 0.0)
                least = jnp.minimum(least, jnp.where(on, found[h], 1.0))
                most = jnp.maximum(most, jnp.where(on, found[h], 1.0))
        return least, most

    one = jnp.ones((1, HALF), jnp.float32)
    return lax.fori_loop(0, (live + size - 1) // size, group, (one, one))


def finish(out, top, total):
    found = total[...] > 0.0
    out[...] = jnp.where(found, top[...] + jnp.log2(jnp.where(found, total[...], 1.0)), FLOOR)


def product(first, second):
    turned = first.T
    turned = jnp.concatenate((turned, turned), axis=1)
    high, middle = second[:DEPTH], second[DEPTH:]
    other = jnp.concatenate((high, high, middle, middle), axis=0)
    return jnp.dot(turned, other, preferred_element_type=jnp.float32)


def cost_kernel(
    blocks_in, blocks_out, tiles_in, counts, src, tgt, cost, out, lefts, rights, tiles,
    tsem, xs, ys, ext, top, total, xsem, ysem
):
    table = pltpu.make_async_copy(tiles_in, tiles, tsem)
    table.start()
    width = src.shape[0]
    ext[...] = jnp.zeros_like(ext)
    for u in range(GROUP):
        for side, place in ((0, 1), (0, 3), (1, 0), (1, 2)):
            ext[u, side, pl.ds(width + place, 1), :] = jnp.ones((1, TILE), jnp.float32)
    top[...] = jnp.full_like(top, FLOOR)
    total[...] = jnp.zeros_like(total)
    table.wait()
    live = counts[0, 0]

    def copies(k):
        first = pl.multiple_of(block(tiles, 0, k, blocks_out) * TILE, TILE)
        second = pl.multiple_of(block(tiles, 1, k, blocks_in) * TILE, TILE)
        return (
            pltpu.make_async_copy(src.at[:, pl.ds(first, TILE)], xs.at[k], xsem.at[k]),
            pltpu.make_async_copy(tgt.at[:, pl.ds(second, TILE)], ys.at[k], ysem.at[k]),
        )

    def begin(k, carry):
        for one in copies(k):
            one.start()
        return carry

    def end(k, carry):
        for one in copies(k):
            one.wait()
        return carry

    lax.fori_loop(0, live, begin, 0)

    def extend(u, side, points, scale):
        square = jnp.sum(points * points, axis=0, keepdims=True) * SCALE
        high, middle = split(square)
        ext[u, side, pl.ds(0, width), :] = points * scale
        ext[u, side, pl.ds(width + side, 1), :] = square
        rest = square - high.astype(jnp.float32) - middle.astype(jnp.float32)
        ext[u, side, pl.ds(width + side + 2, 1), :] = rest
        return jnp.concatenate(split(ext[u, side]), axis=0)

    def group(q, carry):
        lax.fori_loop(q * GROUP, jnp.minimum(live, q * GROUP + GROUP), end, 0)
        ready = []
        for u in range(GROUP):
            k = q * GROUP + u
            centre = ys[k, :, pl.ds(0, 1)]
            left = extend(u, 0, xs[k] - centre, -2.0 * SCALE)
            right = extend(u, 1, ys[k] - centre, 1.0)
            lefts[k] = left
            rights[k] = right
            value = product(right, left)
            cost[k] = value
            peak = 0.0 - jnp.min(value, axis=0, keepdims=True)
            ready.append((k < live, block(tiles, 0, k, blocks_out), peak))
        for on, index, peak in ready:
            for h in range(2):
                new = jnp.where(on, peak[:, h * HALF : (h + 1) * HALF], FLOOR)
                top[row(index, h), :] = jnp.maximum(top[row(index, h), :], new)
        return carry

    lax.fori_loop(0, (live + GROUP - 1) // GROUP, group, 0)
    add_up(WIDE, live, tiles, 0, blocks_out, cost, lambda k: None, top, total)
    finish(out, top, total)


def turn_kernel(counts, lefts, rights, cost):
    live = counts[0, 0]

    def group(q, carry):
        for u in range(GROUP):
            k = q * GROUP + u
            cost[k] = product(lefts[k], rights[k])
        return carry

    lax.fori_loop(0, (live + GROUP - 1) // GROUP, group, 0)


def sweep_kernel(offset, far, last, inner, outer, blocks_in, blocks_out, tiles, counts, cost, *refs):
    parts = refs[:-6]
    out, result, held, top, total, rsem = refs[-6:]
    if far is None:
        top[...] = jnp.full_like(top, offset)
    else:
        top[...] = far - parts[0][...]
        parts = parts[1:]
    potential = offset - lse2_many([part[...] for part in parts])
    held[0] = potential
    if last:
        held[1] = potential / SCALE
        leave = pltpu.make_async_copy(held.at[1], result, rsem)
        leave.start()
    else:
        result[...] = potential
    total[...] = jnp.zeros_like(total)
    live = counts[0, 0]

    def potential_of(k):
        return spread(held, block(tiles, inner, k, blocks_in))

    least, most = add_up(WIDE, live, tiles, outer, blocks_out, cost, potential_of, top, total)
    finish(out, top, total)
    exact = (jnp.min(least) >= LEAST) & (jnp.max(most) <= MOST)

    @pl.when(jnp.logical_not(exact))
    def _():
        top[...] = jnp.full_like(top, FLOOR)
        total[...] = jnp.zeros_like(total)

        def step(k, carry):
            index = block(tiles, outer, k, blocks_out)
            found = peaks(k, cost, potential_of(k))
            for h in range(2):
                top[row(index, h), :] = jnp.maximum(top[row(index, h), :], found[h])
            return carry

        lax.fori_loop(0, live, step, 0)
        add_up(2, live, tiles, outer, blocks_out, cost, potential_of, top, total)
        finish(out, top, total)

    if last:
        leave.wait()


def vmem_spec():
    return pl.BlockSpec(memory_space=pltpu.VMEM)


def smem_spec():
    return pl.BlockSpec(memory_space=pltpu.SMEM)


def hbm_spec():
    return pl.BlockSpec(memory_space=pltpu.HBM)


def costs(tiles, counts, src, tgt, blocks_in, blocks_out):
    slots = tiles.shape[1]
    width = src.shape[0]
    part = pltpu.VMEM((slots, 2 * DEPTH, TILE), jnp.bfloat16)
    return pl.pallas_call(
        functools.partial(cost_kernel, blocks_in, blocks_out),
        out_shape=(
            pltpu.VMEM((slots, TILE, TILE), jnp.float32),
            jax.ShapeDtypeStruct((2 * blocks_out, HALF), jnp.float32),
            part,
            part,
            pltpu.SMEM(tiles.shape, jnp.int32),
        ),
        in_specs=[hbm_spec(), smem_spec(), hbm_spec(), hbm_spec()],
        out_specs=(vmem_spec(), vmem_spec(), vmem_spec(), vmem_spec(), smem_spec()),
        scratch_shapes=[
            pltpu.SemaphoreType.DMA(()),
            pltpu.VMEM((slots, width, TILE), jnp.float32),
            pltpu.VMEM((slots, width, TILE), jnp.float32),
            pltpu.VMEM((GROUP, 2, DEPTH, TILE), jnp.float32),
            pltpu.VMEM((2 * blocks_out, HALF), jnp.float32),
            pltpu.VMEM((2 * blocks_out, HALF), jnp.float32),
            pltpu.SemaphoreType.DMA((slots,)),
            pltpu.SemaphoreType.DMA((slots,)),
        ],
        compiler_params=pltpu.CompilerParams(vmem_limit_bytes=VMEM_LIMIT),
    )(tiles, counts, src, tgt)


def turned(counts, lefts, rights):
    slots = lefts.shape[0]
    return pl.pallas_call(
        turn_kernel,
        out_shape=pltpu.VMEM((slots, TILE, TILE), jnp.float32),
        in_specs=[smem_spec(), vmem_spec(), vmem_spec()],
        out_specs=vmem_spec(),
        compiler_params=pltpu.CompilerParams(vmem_limit_bytes=VMEM_LIMIT),
        cost_estimate=pl.CostEstimate(
            flops=slots * 8 * DEPTH * TILE * TILE, bytes_accessed=slots * 8 * TILE * TILE, transcendentals=0
        ),
    )(counts, lefts, rights)


def sweep(tiles, counts, cost, before, parts, cells, far_cells, inner, outer, blocks_in, blocks_out, last):
    far = None if before is None else math.log2(1.0 / far_cells)
    operands = list(parts) if before is None else [before, *parts]
    kernel = functools.partial(
        sweep_kernel, math.log2(1.0 / cells), far, last, inner, outer, blocks_in, blocks_out
    )
    return pl.pallas_call(
        kernel,
        out_shape=(
            jax.ShapeDtypeStruct((2 * blocks_out, HALF), jnp.float32),
            jax.ShapeDtypeStruct((2 * blocks_in, HALF), jnp.float32),
        ),
        in_specs=[smem_spec(), smem_spec()] + [vmem_spec()] * (1 + len(operands)),
        out_specs=(vmem_spec(), hbm_spec() if last else vmem_spec()),
        scratch_shapes=[
            pltpu.VMEM((2, 2 * blocks_in, HALF), jnp.float32),
            pltpu.VMEM((2 * blocks_out, HALF), jnp.float32),
            pltpu.VMEM((2 * blocks_out, HALF), jnp.float32),
            pltpu.SemaphoreType.DMA(()),
        ],
        compiler_params=pltpu.CompilerParams(vmem_limit_bytes=VMEM_LIMIT),
    )(tiles, counts, cost, *operands)


def swap(value, axis, flips):
    src, tgt = lax.axis_size("src"), lax.axis_size("tgt")
    pairs = []
    for s in range(src):
        for t in range(tgt):
            flip = flips[t % 2]
            other = (s ^ flip, t) if axis == "src" else (s, t ^ flip)
            pairs.append((s * tgt + t, other[0] * tgt + other[1]))
    return lax.ppermute(value, ("src", "tgt"), pairs)


def fan(value, axis, *flips):
    return [value, *[swap(value, axis, each) for each in flips]]


def over_core(value):
    return lse2_many(fan(value, "tgt", (1, 1)))


def over_y(value):
    return fan(value, "tgt", (6, 4), (4, 6), (2, 2))


def over_src(value):
    value = lse2_many(fan(value, "src", (3, 2), (2, 3), (1, 1)))
    for flips in ((4, 4), (12, 28)):
        value = lse2_many(fan(value, "src", flips))
    return fan(value, "src", (28, 12))


def body(src_points, tgt_points, tiles, counts):
    tiles, src_points, tgt_points = (
        pltpu.with_memory_space_constraint(each, pltpu.HBM)
        for each in (tiles[0, 0], src_points, tgt_points)
    )
    row_blocks = src_points.shape[1] // TILE
    col_blocks = tgt_points.shape[1] // TILE
    src_cells = src_points.shape[1] * lax.axis_size("src")
    tgt_cells = tgt_points.shape[1] * lax.axis_size("tgt")
    cost_ba, rows, lefts, rights, tiles = costs(
        tiles, counts, src_points, tgt_points, col_blocks, row_blocks
    )
    target = None
    for turn in range(ITERS):
        last = turn == ITERS - 1
        rows = over_core(rows)
        if turn == 0:
            rows, lefts = lax.optimization_barrier((rows, lefts))
            cost_ab = turned(counts, lefts, rights)
        cols, source = sweep(
            tiles, counts, cost_ab, target, over_y(rows), src_cells, tgt_cells, 0, 1,
            row_blocks, col_blocks, last,
        )
        parts = over_src(cols)
        if last:
            target = (math.log2(1.0 / tgt_cells) - lse2_many(parts)) / SCALE
        else:
            rows, target = sweep(
                tiles, counts, cost_ba, source, parts, tgt_cells, src_cells, 1, 0,
                col_blocks, row_blocks, False,
            )
    return (source.reshape(-1), target.reshape(-1))


def solution(mesh):
    in_specs = (P(None, "src"), P(None, "tgt"), P("src", "tgt", None, None), P("src", "tgt"))
    out_specs = (P("src"), P("tgt"))
    return jax.shard_map(body, mesh=mesh, in_specs=in_specs, out_specs=out_specs, check_vma=False)
```

```python
import functools
import math

import jax
import jax.numpy as jnp
from jax import lax
from jax.experimental import pallas as pl
from jax.experimental.pallas import tpu as pltpu
from jax.sharding import PartitionSpec as P

TILE = 256
HALF = 128
ROWS = 8
GROUP = 8
WIDE = 16
ITERS = 3
EPS = 0.05
FLOOR = -1e30
SCALE = 1.0 / (EPS * math.log(2.0))
DEPTH = 64
LEAST = 2.0**-80
MOST = 2.0**100
VMEM_LIMIT = 16 * 1024 * 1024


def lse2_many(parts):
    top = functools.reduce(jnp.maximum, parts)
    return top + jnp.log2(functools.reduce(jnp.add, [jnp.exp2(p - top) for p in parts]))


def split(value):
    high = value.astype(jnp.bfloat16)
    return high, (value - high.astype(jnp.float32)).astype(jnp.bfloat16)


def halves():
    return [(h, pl.ds(h * HALF, HALF)) for h in range(2)]


def row(index, h):
    return pl.ds(2 * index + h, 1)


def block(tiles, side, k, blocks):
    return jnp.minimum(tiles[side, k], blocks - 1)


def sums(k, cost, potential, shift):
    found = []
    for h, lanes in halves():
        kept = None
        for g, cells in halves():
            score = cost[k, cells, lanes]
            score = (0.0 - score if potential is None else potential[g] - score) - shift[h]
            part = jnp.sum(jnp.exp2(score).reshape(HALF // ROWS, ROWS, HALF), axis=0)
            kept = part if kept is None else kept + part
        found.append(jnp.sum(kept, axis=0, keepdims=True))
    return found


def peaks(k, cost, potential):
    found = []
    for h, lanes in halves():
        kept = None
        for g, cells in halves():
            score = cost[k, cells, lanes]
            score = 0.0 - score if potential is None else potential[g] - score
            part = jnp.max(score, axis=0, keepdims=True)
            kept = part if kept is None else jnp.maximum(kept, part)
        found.append(kept)
    return found


def spread(held, index):
    return [jnp.broadcast_to(held[0, row(index, g), :], (HALF, HALF)).T for g in range(2)]


def add_up(size, live, tiles, outer, blocks_out, cost, potential_of, top, total):
    def group(q, carry):
        least, most = carry
        ready = []
        for u in range(size):
            k = q * size + u
            out = block(tiles, outer, k, blocks_out)
            shift = [top[row(out, h), :] for h in range(2)]
            ready.append((k < live, out, sums(k, cost, potential_of(k), shift)))
        for on, out, found in ready:
            for h in range(2):
                total[row(out, h), :] = total[row(out, h), :] + jnp.where(on, found[h], 0.0)
                least = jnp.minimum(least, jnp.where(on, found[h], 1.0))
                most = jnp.maximum(most, jnp.where(on, found[h], 1.0))
        return least, most

    one = jnp.ones((1, HALF), jnp.float32)
    return lax.fori_loop(0, (live + size - 1) // size, group, (one, one))


def finish(out, top, total):
    found = total[...] > 0.0
    out[...] = jnp.where(found, top[...] + jnp.log2(jnp.where(found, total[...], 1.0)), FLOOR)


def product(first, second):
    turned = first.T
    turned = jnp.concatenate((turned, turned), axis=1)
    high, middle = second[:DEPTH], second[DEPTH:]
    other = jnp.concatenate((high, high, middle, middle), axis=0)
    return jnp.dot(turned, other, preferred_element_type=jnp.float32)


def cost_kernel(
    blocks_in, blocks_out, tiles_in, counts, src, tgt, cost, out, lefts, rights, tiles,
    tsem, xs, ys, ext, top, total, xsem, ysem
):
    table = pltpu.make_async_copy(tiles_in, tiles, tsem)
    table.start()
    width = src.shape[0]
    ext[...] = jnp.zeros_like(ext)
    for u in range(GROUP):
        for side, place in ((0, 1), (0, 3), (1, 0), (1, 2)):
            ext[u, side, pl.ds(width + place, 1), :] = jnp.ones((1, TILE), jnp.float32)
    top[...] = jnp.full_like(top, FLOOR)
    total[...] = jnp.zeros_like(total)
    table.wait()
    live = counts[0, 0]

    def copies(k):
        first = pl.multiple_of(block(tiles, 0, k, blocks_out) * TILE, TILE)
        second = pl.multiple_of(block(tiles, 1, k, blocks_in) * TILE, TILE)
        return (
            pltpu.make_async_copy(src.at[:, pl.ds(first, TILE)], xs.at[k], xsem.at[k]),
            pltpu.make_async_copy(tgt.at[:, pl.ds(second, TILE)], ys.at[k], ysem.at[k]),
        )

    def begin(k, carry):
        for one in copies(k):
            one.start()
        return carry

    def end(k, carry):
        for one in copies(k):
            one.wait()
        return carry

    lax.fori_loop(0, live, begin, 0)

    def extend(u, side, points, scale):
        square = jnp.sum(points * points, axis=0, keepdims=True) * SCALE
        high, middle = split(square)
        ext[u, side, pl.ds(0, width), :] = points * scale
        ext[u, side, pl.ds(width + side, 1), :] = square
        rest = square - high.astype(jnp.float32) - middle.astype(jnp.float32)
        ext[u, side, pl.ds(width + side + 2, 1), :] = rest
        return jnp.concatenate(split(ext[u, side]), axis=0)

    def group(q, carry):
        lax.fori_loop(q * GROUP, jnp.minimum(live, q * GROUP + GROUP), end, 0)
        ready = []
        for u in range(GROUP):
            k = q * GROUP + u
            centre = ys[k, :, pl.ds(0, 1)]
            left = extend(u, 0, xs[k] - centre, -2.0 * SCALE)
            right = extend(u, 1, ys[k] - centre, 1.0)
            lefts[k] = left
            rights[k] = right
            value = product(right, left)
            cost[k] = value
            peak = 0.0 - jnp.min(value, axis=0, keepdims=True)
            ready.append((k < live, block(tiles, 0, k, blocks_out), peak))
        for on, index, peak in ready:
            for h in range(2):
                new = jnp.where(on, peak[:, h * HALF : (h + 1) * HALF], FLOOR)
                top[row(index, h), :] = jnp.maximum(top[row(index, h), :], new)
        return carry

    lax.fori_loop(0, (live + GROUP - 1) // GROUP, group, 0)
    add_up(WIDE, live, tiles, 0, blocks_out, cost, lambda k: None, top, total)
    finish(out, top, total)


def turn_kernel(counts, lefts, rights, cost):
    live = counts[0, 0]

    def group(q, carry):
        for u in range(GROUP):
            k = q * GROUP + u
            cost[k] = product(lefts[k], rights[k])
        return carry

    lax.fori_loop(0, (live + GROUP - 1) // GROUP, group, 0)


def sweep_kernel(offset, far, last, inner, outer, blocks_in, blocks_out, tiles, counts, cost, *refs):
    parts = refs[:-6]
    out, result, held, top, total, rsem = refs[-6:]
    if far is None:
        top[...] = jnp.full_like(top, offset)
    else:
        top[...] = far - parts[0][...]
        parts = parts[1:]
    potential = offset - lse2_many([part[...] for part in parts])
    held[0] = potential
    if last:
        held[1] = potential / SCALE
        leave = pltpu.make_async_copy(held.at[1], result, rsem)
        leave.start()
    else:
        result[...] = potential
    total[...] = jnp.zeros_like(total)
    live = counts[0, 0]

    def potential_of(k):
        return spread(held, block(tiles, inner, k, blocks_in))

    least, most = add_up(WIDE, live, tiles, outer, blocks_out, cost, potential_of, top, total)
    finish(out, top, total)
    exact = (jnp.min(least) >= LEAST) & (jnp.max(most) <= MOST)

    @pl.when(jnp.logical_not(exact))
    def _():
        top[...] = jnp.full_like(top, FLOOR)
        total[...] = jnp.zeros_like(total)

        def step(k, carry):
            index = block(tiles, outer, k, blocks_out)
            found = peaks(k, cost, potential_of(k))
            for h in range(2):
                top[row(index, h), :] = jnp.maximum(top[row(index, h), :], found[h])
            return carry

        lax.fori_loop(0, live, step, 0)
        add_up(2, live, tiles, outer, blocks_out, cost, potential_of, top, total)
        finish(out, top, total)

    if last:
        leave.wait()


def vmem_spec():
    return pl.BlockSpec(memory_space=pltpu.VMEM)


def smem_spec():
    return pl.BlockSpec(memory_space=pltpu.SMEM)


def hbm_spec():
    return pl.BlockSpec(memory_space=pltpu.HBM)


def costs(tiles, counts, src, tgt, blocks_in, blocks_out):
    slots = tiles.shape[1]
    width = src.shape[0]
    part = pltpu.VMEM((slots, 2 * DEPTH, TILE), jnp.bfloat16)
    return pl.pallas_call(
        functools.partial(cost_kernel, blocks_in, blocks_out),
        out_shape=(
            pltpu.VMEM((slots, TILE, TILE), jnp.float32),
            jax.ShapeDtypeStruct((2 * blocks_out, HALF), jnp.float32),
            part,
            part,
            pltpu.SMEM(tiles.shape, jnp.int32),
        ),
        in_specs=[hbm_spec(), smem_spec(), hbm_spec(), hbm_spec()],
        out_specs=(vmem_spec(), vmem_spec(), vmem_spec(), vmem_spec(), smem_spec()),
        scratch_shapes=[
            pltpu.SemaphoreType.DMA(()),
            pltpu.VMEM((slots, width, TILE), jnp.float32),
            pltpu.VMEM((slots, width, TILE), jnp.float32),
            pltpu.VMEM((GROUP, 2, DEPTH, TILE), jnp.float32),
            pltpu.VMEM((2 * blocks_out, HALF), jnp.float32),
            pltpu.VMEM((2 * blocks_out, HALF), jnp.float32),
            pltpu.SemaphoreType.DMA((slots,)),
            pltpu.SemaphoreType.DMA((slots,)),
        ],
        compiler_params=pltpu.CompilerParams(vmem_limit_bytes=VMEM_LIMIT),
    )(tiles, counts, src, tgt)


def turned(counts, lefts, rights):
    slots = lefts.shape[0]
    return pl.pallas_call(
        turn_kernel,
        out_shape=pltpu.VMEM((slots, TILE, TILE), jnp.float32),
        in_specs=[smem_spec(), vmem_spec(), vmem_spec()],
        out_specs=vmem_spec(),
        compiler_params=pltpu.CompilerParams(vmem_limit_bytes=VMEM_LIMIT),
        cost_estimate=pl.CostEstimate(
            flops=slots * 8 * DEPTH * TILE * TILE, bytes_accessed=slots * 8 * TILE * TILE, transcendentals=0
        ),
    )(counts, lefts, rights)


def sweep(tiles, counts, cost, before, parts, cells, far_cells, inner, outer, blocks_in, blocks_out, last):
    far = None if before is None else math.log2(1.0 / far_cells)
    operands = list(parts) if before is None else [before, *parts]
    kernel = functools.partial(
        sweep_kernel, math.log2(1.0 / cells), far, last, inner, outer, blocks_in, blocks_out
    )
    return pl.pallas_call(
        kernel,
        out_shape=(
            jax.ShapeDtypeStruct((2 * blocks_out, HALF), jnp.float32),
            jax.ShapeDtypeStruct((2 * blocks_in, HALF), jnp.float32),
        ),
        in_specs=[smem_spec(), smem_spec()] + [vmem_spec()] * (1 + len(operands)),
        out_specs=(vmem_spec(), hbm_spec() if last else vmem_spec()),
        scratch_shapes=[
            pltpu.VMEM((2, 2 * blocks_in, HALF), jnp.float32),
            pltpu.VMEM((2 * blocks_out, HALF), jnp.float32),
            pltpu.VMEM((2 * blocks_out, HALF), jnp.float32),
            pltpu.SemaphoreType.DMA(()),
        ],
        compiler_params=pltpu.CompilerParams(vmem_limit_bytes=VMEM_LIMIT),
    )(tiles, counts, cost, *operands)


def swap(value, axis, flips):
    src, tgt = lax.axis_size("src"), lax.axis_size("tgt")
    pairs = []
    for s in range(src):
        for t in range(tgt):
            flip = flips[t % 2]
            other = (s ^ flip, t) if axis == "src" else (s, t ^ flip)
            pairs.append((s * tgt + t, other[0] * tgt + other[1]))
    return lax.ppermute(value, ("src", "tgt"), pairs)


def fan(value, axis, *flips):
    return [value, *[swap(value, axis, each) for each in flips]]


def over_y(value):
    return lse2_many(fan(value, "tgt", (2, 2), (4, 4), (6, 6)))


def over_core(value):
    return fan(value, "tgt", (1, 1))


def over_src(value):
    value = lse2_many(fan(value, "src", (1, 1), (2, 2), (3, 3)))
    for flips in ((4, 4), (12, 28)):
        value = lse2_many(fan(value, "src", flips))
    return fan(value, "src", (28, 12))


def body(src_points, tgt_points, tiles, counts):
    tiles, src_points, tgt_points = (
        pltpu.with_memory_space_constraint(each, pltpu.HBM)
        for each in (tiles[0, 0], src_points, tgt_points)
    )
    row_blocks = src_points.shape[1] // TILE
    col_blocks = tgt_points.shape[1] // TILE
    src_cells = src_points.shape[1] * lax.axis_size("src")
    tgt_cells = tgt_points.shape[1] * lax.axis_size("tgt")
    cost_ba, rows, lefts, rights, tiles = costs(
        tiles, counts, src_points, tgt_points, col_blocks, row_blocks
    )
    target = None
    for turn in range(ITERS):
        last = turn == ITERS - 1
        rows = over_y(rows)
        if turn == 0:
            cost_ab = turned(counts, lefts, rights)
            rows, cost_ab = lax.optimization_barrier((rows, cost_ab))
        cols, source = sweep(
            tiles, counts, cost_ab, target, over_core(rows), src_cells, tgt_cells, 0, 1,
            row_blocks, col_blocks, last,
        )
        parts = over_src(cols)
        if last:
            target = (math.log2(1.0 / tgt_cells) - lse2_many(parts)) / SCALE
        else:
            rows, target = sweep(
                tiles, counts, cost_ba, source, parts, tgt_cells, src_cells, 1, 0,
                col_blocks, row_blocks, False,
            )
    return (source.reshape(-1), target.reshape(-1))


def solution(mesh):
    in_specs = (P(None, "src"), P(None, "tgt"), P("src", "tgt", None, None), P("src", "tgt"))
    out_specs = (P("src"), P("tgt"))
    return jax.shard_map(body, mesh=mesh, in_specs=in_specs, out_specs=out_specs, check_vma=False)
```

```python
import functools
import math

import jax
import jax.numpy as jnp
from jax import lax
from jax.experimental import pallas as pl
from jax.experimental.pallas import tpu as pltpu
from jax.sharding import PartitionSpec as P

TILE = 256
HALF = 128
ROWS = 8
GROUP = 8
WIDE = 16
ITERS = 3
EPS = 0.05
FLOOR = -1e30
SCALE = 1.0 / (EPS * math.log(2.0))
DEPTH = 64
LEAST = 2.0**-80
MOST = 2.0**100
VMEM_LIMIT = 16 * 1024 * 1024


def lse2_many(parts):
    top = functools.reduce(jnp.maximum, parts)
    return top + jnp.log2(functools.reduce(jnp.add, [jnp.exp2(p - top) for p in parts]))


def split(value):
    high = value.astype(jnp.bfloat16)
    return high, (value - high.astype(jnp.float32)).astype(jnp.bfloat16)


def halves():
    return [(h, pl.ds(h * HALF, HALF)) for h in range(2)]


def row(index, h):
    return pl.ds(2 * index + h, 1)


def block(tiles, side, k, blocks):
    return jnp.minimum(tiles[side, k], blocks - 1)


def sums(k, cost, potential, shift):
    found = []
    for h, lanes in halves():
        kept = None
        for g, cells in halves():
            score = cost[k, cells, lanes]
            score = (0.0 - score if potential is None else potential[g] - score) - shift[h]
            part = jnp.sum(jnp.exp2(score).reshape(HALF // ROWS, ROWS, HALF), axis=0)
            kept = part if kept is None else kept + part
        found.append(jnp.sum(kept, axis=0, keepdims=True))
    return found


def peaks(k, cost, potential):
    found = []
    for h, lanes in halves():
        kept = None
        for g, cells in halves():
            score = cost[k, cells, lanes]
            score = 0.0 - score if potential is None else potential[g] - score
            part = jnp.max(score, axis=0, keepdims=True)
            kept = part if kept is None else jnp.maximum(kept, part)
        found.append(kept)
    return found


def spread(held, index):
    return [jnp.broadcast_to(held[0, row(index, g), :], (HALF, HALF)).T for g in range(2)]


def add_up(size, live, tiles, outer, blocks_out, cost, potential_of, top, total):
    def group(q, carry):
        least, most = carry
        ready = []
        for u in range(size):
            k = q * size + u
            out = block(tiles, outer, k, blocks_out)
            shift = [top[row(out, h), :] for h in range(2)]
            ready.append((k < live, out, sums(k, cost, potential_of(k), shift)))
        for on, out, found in ready:
            for h in range(2):
                total[row(out, h), :] = total[row(out, h), :] + jnp.where(on, found[h], 0.0)
                least = jnp.minimum(least, jnp.where(on, found[h], 1.0))
                most = jnp.maximum(most, jnp.where(on, found[h], 1.0))
        return least, most

    one = jnp.ones((1, HALF), jnp.float32)
    return lax.fori_loop(0, (live + size - 1) // size, group, (one, one))


def finish(out, top, total):
    found = total[...] > 0.0
    out[...] = jnp.where(found, top[...] + jnp.log2(jnp.where(found, total[...], 1.0)), FLOOR)


def product(first, second):
    turned = first.T
    turned = jnp.concatenate((turned, turned), axis=1)
    high, middle = second[:DEPTH], second[DEPTH:]
    other = jnp.concatenate((high, high, middle, middle), axis=0)
    return jnp.dot(turned, other, preferred_element_type=jnp.float32)


def cost_kernel(
    blocks_in, blocks_out, tiles_in, counts, src, tgt, cost, out, lefts, rights, tiles,
    tsem, xs, ys, ext, top, total, xsem, ysem
):
    table = pltpu.make_async_copy(tiles_in, tiles, tsem)
    table.start()
    width = src.shape[0]
    ext[...] = jnp.zeros_like(ext)
    for u in range(GROUP):
        for side, place in ((0, 1), (0, 3), (1, 0), (1, 2)):
            ext[u, side, pl.ds(width + place, 1), :] = jnp.ones((1, TILE), jnp.float32)
    top[...] = jnp.full_like(top, FLOOR)
    total[...] = jnp.zeros_like(total)
    table.wait()
    live = counts[0, 0]

    def copies(k):
        first = pl.multiple_of(block(tiles, 0, k, blocks_out) * TILE, TILE)
        second = pl.multiple_of(block(tiles, 1, k, blocks_in) * TILE, TILE)
        return (
            pltpu.make_async_copy(src.at[:, pl.ds(first, TILE)], xs.at[k], xsem.at[k]),
            pltpu.make_async_copy(tgt.at[:, pl.ds(second, TILE)], ys.at[k], ysem.at[k]),
        )

    def begin(k, carry):
        for one in copies(k):
            one.start()
        return carry

    def end(k, carry):
        for one in copies(k):
            one.wait()
        return carry

    lax.fori_loop(0, live, begin, 0)

    def extend(u, side, points, scale):
        square = jnp.sum(points * points, axis=0, keepdims=True) * SCALE
        high, middle = split(square)
        ext[u, side, pl.ds(0, width), :] = points * scale
        ext[u, side, pl.ds(width + side, 1), :] = square
        rest = square - high.astype(jnp.float32) - middle.astype(jnp.float32)
        ext[u, side, pl.ds(width + side + 2, 1), :] = rest
        return jnp.concatenate(split(ext[u, side]), axis=0)

    def group(q, carry):
        lax.fori_loop(q * GROUP, jnp.minimum(live, q * GROUP + GROUP), end, 0)
        ready = []
        for u in range(GROUP):
            k = q * GROUP + u
            centre = ys[k, :, pl.ds(0, 1)]
            left = extend(u, 0, xs[k] - centre, -2.0 * SCALE)
            right = extend(u, 1, ys[k] - centre, 1.0)
            lefts[k] = left
            rights[k] = right
            value = product(right, left)
            cost[k] = value
            peak = 0.0 - jnp.min(value, axis=0, keepdims=True)
            ready.append((k < live, block(tiles, 0, k, blocks_out), peak))
        for on, index, peak in ready:
            for h in range(2):
                new = jnp.where(on, peak[:, h * HALF : (h + 1) * HALF], FLOOR)
                top[row(index, h), :] = jnp.maximum(top[row(index, h), :], new)
        return carry

    lax.fori_loop(0, (live + GROUP - 1) // GROUP, group, 0)
    add_up(WIDE, live, tiles, 0, blocks_out, cost, lambda k: None, top, total)
    finish(out, top, total)


def turn_kernel(counts, lefts, rights, cost):
    live = counts[0, 0]

    def group(q, carry):
        for u in range(GROUP):
            k = q * GROUP + u
            cost[k] = product(lefts[k], rights[k])
        return carry

    lax.fori_loop(0, (live + GROUP - 1) // GROUP, group, 0)


def sweep_kernel(offset, far, last, inner, outer, blocks_in, blocks_out, tiles, counts, cost, *refs):
    parts = refs[:-6]
    out, result, held, top, total, rsem = refs[-6:]
    if far is None:
        top[...] = jnp.full_like(top, offset)
    else:
        top[...] = far - parts[0][...]
        parts = parts[1:]
    potential = offset - lse2_many([part[...] for part in parts])
    held[0] = potential
    if last:
        held[1] = potential / SCALE
        leave = pltpu.make_async_copy(held.at[1], result, rsem)
        leave.start()
    else:
        result[...] = potential
    total[...] = jnp.zeros_like(total)
    live = counts[0, 0]

    def potential_of(k):
        return spread(held, block(tiles, inner, k, blocks_in))

    least, most = add_up(WIDE, live, tiles, outer, blocks_out, cost, potential_of, top, total)
    finish(out, top, total)
    exact = (jnp.min(least) >= LEAST) & (jnp.max(most) <= MOST)

    @pl.when(jnp.logical_not(exact))
    def _():
        top[...] = jnp.full_like(top, FLOOR)
        total[...] = jnp.zeros_like(total)

        def step(k, carry):
            index = block(tiles, outer, k, blocks_out)
            found = peaks(k, cost, potential_of(k))
            for h in range(2):
                top[row(index, h), :] = jnp.maximum(top[row(index, h), :], found[h])
            return carry

        lax.fori_loop(0, live, step, 0)
        add_up(2, live, tiles, outer, blocks_out, cost, potential_of, top, total)
        finish(out, top, total)

    if last:
        leave.wait()


def vmem_spec():
    return pl.BlockSpec(memory_space=pltpu.VMEM)


def smem_spec():
    return pl.BlockSpec(memory_space=pltpu.SMEM)


def hbm_spec():
    return pl.BlockSpec(memory_space=pltpu.HBM)


def costs(tiles, counts, src, tgt, blocks_in, blocks_out):
    slots = tiles.shape[1]
    width = src.shape[0]
    part = pltpu.VMEM((slots, 2 * DEPTH, TILE), jnp.bfloat16)
    return pl.pallas_call(
        functools.partial(cost_kernel, blocks_in, blocks_out),
        out_shape=(
            pltpu.VMEM((slots, TILE, TILE), jnp.float32),
            jax.ShapeDtypeStruct((2 * blocks_out, HALF), jnp.float32),
            part,
            part,
            pltpu.SMEM(tiles.shape, jnp.int32),
        ),
        in_specs=[hbm_spec(), smem_spec(), hbm_spec(), hbm_spec()],
        out_specs=(vmem_spec(), vmem_spec(), vmem_spec(), vmem_spec(), smem_spec()),
        scratch_shapes=[
            pltpu.SemaphoreType.DMA(()),
            pltpu.VMEM((slots, width, TILE), jnp.float32),
            pltpu.VMEM((slots, width, TILE), jnp.float32),
            pltpu.VMEM((GROUP, 2, DEPTH, TILE), jnp.float32),
            pltpu.VMEM((2 * blocks_out, HALF), jnp.float32),
            pltpu.VMEM((2 * blocks_out, HALF), jnp.float32),
            pltpu.SemaphoreType.DMA((slots,)),
            pltpu.SemaphoreType.DMA((slots,)),
        ],
        compiler_params=pltpu.CompilerParams(vmem_limit_bytes=VMEM_LIMIT),
    )(tiles, counts, src, tgt)


def turned(counts, lefts, rights):
    slots = lefts.shape[0]
    return pl.pallas_call(
        turn_kernel,
        out_shape=pltpu.VMEM((slots, TILE, TILE), jnp.float32),
        in_specs=[smem_spec(), vmem_spec(), vmem_spec()],
        out_specs=vmem_spec(),
        compiler_params=pltpu.CompilerParams(vmem_limit_bytes=VMEM_LIMIT),
        cost_estimate=pl.CostEstimate(
            flops=slots * 8 * DEPTH * TILE * TILE, bytes_accessed=slots * 8 * TILE * TILE, transcendentals=0
        ),
    )(counts, lefts, rights)


def sweep(tiles, counts, cost, before, parts, cells, far_cells, inner, outer, blocks_in, blocks_out, last):
    far = None if before is None else math.log2(1.0 / far_cells)
    operands = list(parts) if before is None else [before, *parts]
    kernel = functools.partial(
        sweep_kernel, math.log2(1.0 / cells), far, last, inner, outer, blocks_in, blocks_out
    )
    return pl.pallas_call(
        kernel,
        out_shape=(
            jax.ShapeDtypeStruct((2 * blocks_out, HALF), jnp.float32),
            jax.ShapeDtypeStruct((2 * blocks_in, HALF), jnp.float32),
        ),
        in_specs=[smem_spec(), smem_spec()] + [vmem_spec()] * (1 + len(operands)),
        out_specs=(vmem_spec(), hbm_spec() if last else vmem_spec()),
        scratch_shapes=[
            pltpu.VMEM((2, 2 * blocks_in, HALF), jnp.float32),
            pltpu.VMEM((2 * blocks_out, HALF), jnp.float32),
            pltpu.VMEM((2 * blocks_out, HALF), jnp.float32),
            pltpu.SemaphoreType.DMA(()),
        ],
        compiler_params=pltpu.CompilerParams(vmem_limit_bytes=VMEM_LIMIT),
    )(tiles, counts, cost, *operands)


def swap(value, axis, flips):
    src, tgt = lax.axis_size("src"), lax.axis_size("tgt")
    pairs = []
    for s in range(src):
        for t in range(tgt):
            flip = flips[t % 2]
            other = (s ^ flip, t) if axis == "src" else (s, t ^ flip)
            pairs.append((s * tgt + t, other[0] * tgt + other[1]))
    return lax.ppermute(value, ("src", "tgt"), pairs)


def fan(value, axis, *flips):
    return [value, *[swap(value, axis, each) for each in flips]]


def over_core(value):
    return lse2_many(fan(value, "tgt", (1, 1)))


def over_y(value):
    return fan(value, "tgt", (6, 4), (4, 6), (2, 2))


def hand(value, giver):
    src, tgt = lax.axis_size("src"), lax.axis_size("tgt")
    pairs = [(s * tgt + t, s * tgt + (t ^ 1)) for s in range(src) for t in range(giver, tgt, 2)]
    return lax.ppermute(value, ("src", "tgt"), pairs)


def among(value, *flips):
    src, tgt = lax.axis_size("src"), lax.axis_size("tgt")
    got = [value]
    for flip in flips:
        pairs = [(s * tgt + t, (s ^ flip) * tgt + t) for s in range(src) for t in range(1, tgt, 2)]
        got.append(lax.ppermute(value, ("src", "tgt"), pairs))
    return got


def over_src(value):
    rows = value.shape[0]
    second = lax.axis_index("tgt") % 2 == 1
    both = jnp.concatenate([value, hand(value, 0)], axis=0)
    for flips in ((3, 2, 1), (4,), (12,)):
        both = lse2_many(among(both, *flips))
    parts = among(both, 28)
    own = lse2_many([part[:rows] for part in parts])
    other = hand(lse2_many([part[rows:] for part in parts]), 1)
    return [jnp.where(second, own, other)]


def body(src_points, tgt_points, tiles, counts):
    tiles, src_points, tgt_points = (
        pltpu.with_memory_space_constraint(each, pltpu.HBM)
        for each in (tiles[0, 0], src_points, tgt_points)
    )
    row_blocks = src_points.shape[1] // TILE
    col_blocks = tgt_points.shape[1] // TILE
    src_cells = src_points.shape[1] * lax.axis_size("src")
    tgt_cells = tgt_points.shape[1] * lax.axis_size("tgt")
    cost_ba, rows, lefts, rights, tiles = costs(
        tiles, counts, src_points, tgt_points, col_blocks, row_blocks
    )
    target = None
    for turn in range(ITERS):
        last = turn == ITERS - 1
        rows = over_core(rows)
        if turn == 0:
            rows, lefts = lax.optimization_barrier((rows, lefts))
            cost_ab = turned(counts, lefts, rights)
        cols, source = sweep(
            tiles, counts, cost_ab, target, over_y(rows), src_cells, tgt_cells, 0, 1,
            row_blocks, col_blocks, last,
        )
        parts = over_src(cols)
        if last:
            target = (math.log2(1.0 / tgt_cells) - lse2_many(parts)) / SCALE
        else:
            rows, target = sweep(
                tiles, counts, cost_ba, source, parts, tgt_cells, src_cells, 1, 0,
                col_blocks, row_blocks, False,
            )
    return (source.reshape(-1), target.reshape(-1))


def solution(mesh):
    in_specs = (P(None, "src"), P(None, "tgt"), P("src", "tgt", None, None), P("src", "tgt"))
    out_specs = (P("src"), P("tgt"))
    return jax.shard_map(body, mesh=mesh, in_specs=in_specs, out_specs=out_specs, check_vma=False)
```

```python
import functools
import math

import jax
import jax.numpy as jnp
from jax import lax
from jax.experimental import pallas as pl
from jax.experimental.pallas import tpu as pltpu
from jax.sharding import PartitionSpec as P

TILE = 256
HALF = 128
ROWS = 8
GROUP = 8
WIDE = 16
ITERS = 3
EPS = 0.05
FLOOR = -1e30
SCALE = 1.0 / (EPS * math.log(2.0))
DEPTH = 64
LEAST = 2.0**-80
MOST = 2.0**100
VMEM_LIMIT = 16 * 1024 * 1024


def lse2_many(parts):
    top = functools.reduce(jnp.maximum, parts)
    return top + jnp.log2(functools.reduce(jnp.add, [jnp.exp2(p - top) for p in parts]))


def split(value):
    high = value.astype(jnp.bfloat16)
    return high, (value - high.astype(jnp.float32)).astype(jnp.bfloat16)


def halves():
    return [(h, pl.ds(h * HALF, HALF)) for h in range(2)]


def row(index, h):
    return pl.ds(2 * index + h, 1)


def block(tiles, side, k, blocks):
    return jnp.minimum(tiles[side, k], blocks - 1)


def sums(k, cost, potential, shift):
    found = []
    for h, lanes in halves():
        kept = None
        for g, cells in halves():
            score = cost[k, cells, lanes]
            score = (0.0 - score if potential is None else potential[g] - score) - shift[h]
            part = jnp.sum(jnp.exp2(score).reshape(HALF // ROWS, ROWS, HALF), axis=0)
            kept = part if kept is None else kept + part
        found.append(jnp.sum(kept, axis=0, keepdims=True))
    return found


def peaks(k, cost, potential):
    found = []
    for h, lanes in halves():
        kept = None
        for g, cells in halves():
            score = cost[k, cells, lanes]
            score = 0.0 - score if potential is None else potential[g] - score
            part = jnp.max(score, axis=0, keepdims=True)
            kept = part if kept is None else jnp.maximum(kept, part)
        found.append(kept)
    return found


def spread(held, index):
    return [jnp.broadcast_to(held[0, row(index, g), :], (HALF, HALF)).T for g in range(2)]


def add_up(size, live, tiles, outer, blocks_out, cost, potential_of, top, total):
    def group(q, carry):
        least, most = carry
        ready = []
        for u in range(size):
            k = q * size + u
            out = block(tiles, outer, k, blocks_out)
            shift = [top[row(out, h), :] for h in range(2)]
            ready.append((k < live, out, sums(k, cost, potential_of(k), shift)))
        for on, out, found in ready:
            for h in range(2):
                total[row(out, h), :] = total[row(out, h), :] + jnp.where(on, found[h], 0.0)
                least = jnp.minimum(least, jnp.where(on, found[h], 1.0))
                most = jnp.maximum(most, jnp.where(on, found[h], 1.0))
        return least, most

    one = jnp.ones((1, HALF), jnp.float32)
    return lax.fori_loop(0, (live + size - 1) // size, group, (one, one))


def finish(out, top, total):
    found = total[...] > 0.0
    out[...] = jnp.where(found, top[...] + jnp.log2(jnp.where(found, total[...], 1.0)), FLOOR)


def product(first, second):
    turned = first.T
    turned = jnp.concatenate((turned, turned), axis=1)
    high, middle = second[:DEPTH], second[DEPTH:]
    other = jnp.concatenate((high, high, middle, middle), axis=0)
    return jnp.dot(turned, other, preferred_element_type=jnp.float32)


def cost_kernel(
    blocks_in, blocks_out, tiles_in, counts, src, tgt, cost, out, lefts, rights, tiles,
    tsem, xs, ys, ext, top, total, xsem, ysem
):
    table = pltpu.make_async_copy(tiles_in, tiles, tsem)
    table.start()
    width = src.shape[0]
    ext[...] = jnp.zeros_like(ext)
    for u in range(GROUP):
        for side, place in ((0, 1), (0, 3), (1, 0), (1, 2)):
            ext[u, side, pl.ds(width + place, 1), :] = jnp.ones((1, TILE), jnp.float32)
    top[...] = jnp.full_like(top, FLOOR)
    total[...] = jnp.zeros_like(total)
    table.wait()
    live = counts[0, 0]

    def copies(k):
        first = pl.multiple_of(block(tiles, 0, k, blocks_out) * TILE, TILE)
        second = pl.multiple_of(block(tiles, 1, k, blocks_in) * TILE, TILE)
        return (
            pltpu.make_async_copy(src.at[:, pl.ds(first, TILE)], xs.at[k], xsem.at[k]),
            pltpu.make_async_copy(tgt.at[:, pl.ds(second, TILE)], ys.at[k], ysem.at[k]),
        )

    def begin(k, carry):
        for one in copies(k):
            one.start()
        return carry

    def end(k, carry):
        for one in copies(k):
            one.wait()
        return carry

    lax.fori_loop(0, live, begin, 0)

    def extend(u, side, points, scale):
        square = jnp.sum(points * points, axis=0, keepdims=True) * SCALE
        high, middle = split(square)
        ext[u, side, pl.ds(0, width), :] = points * scale
        ext[u, side, pl.ds(width + side, 1), :] = square
        rest = square - high.astype(jnp.float32) - middle.astype(jnp.float32)
        ext[u, side, pl.ds(width + side + 2, 1), :] = rest
        return jnp.concatenate(split(ext[u, side]), axis=0)

    def group(q, carry):
        lax.fori_loop(q * GROUP, jnp.minimum(live, q * GROUP + GROUP), end, 0)
        ready = []
        for u in range(GROUP):
            k = q * GROUP + u
            centre = ys[k, :, pl.ds(0, 1)]
            left = extend(u, 0, xs[k] - centre, -2.0 * SCALE)
            right = extend(u, 1, ys[k] - centre, 1.0)
            lefts[k] = left
            rights[k] = right
            value = product(right, left)
            cost[k] = value
            peak = 0.0 - jnp.min(value, axis=0, keepdims=True)
            ready.append((k < live, block(tiles, 0, k, blocks_out), peak))
        for on, index, peak in ready:
            for h in range(2):
                new = jnp.where(on, peak[:, h * HALF : (h + 1) * HALF], FLOOR)
                top[row(index, h), :] = jnp.maximum(top[row(index, h), :], new)
        return carry

    lax.fori_loop(0, (live + GROUP - 1) // GROUP, group, 0)
    add_up(WIDE, live, tiles, 0, blocks_out, cost, lambda k: None, top, total)
    finish(out, top, total)


def turn_kernel(counts, lefts, rights, cost):
    live = counts[0, 0]

    def group(q, carry):
        for u in range(GROUP):
            k = q * GROUP + u
            cost[k] = product(lefts[k], rights[k])
        return carry

    lax.fori_loop(0, (live + GROUP - 1) // GROUP, group, 0)


def sweep_kernel(offset, far, last, inner, outer, blocks_in, blocks_out, tiles, counts, cost, *refs):
    parts = refs[:-6]
    out, result, held, top, total, rsem = refs[-6:]
    if far is None:
        top[...] = jnp.full_like(top, offset)
    else:
        top[...] = far - parts[0][...]
        parts = parts[1:]
    potential = offset - lse2_many([part[...] for part in parts])
    held[0] = potential
    if last:
        held[1] = potential / SCALE
        leave = pltpu.make_async_copy(held.at[1], result, rsem)
        leave.start()
    else:
        result[...] = potential
    total[...] = jnp.zeros_like(total)
    live = counts[0, 0]

    def potential_of(k):
        return spread(held, block(tiles, inner, k, blocks_in))

    least, most = add_up(WIDE, live, tiles, outer, blocks_out, cost, potential_of, top, total)
    finish(out, top, total)
    exact = (jnp.min(least) >= LEAST) & (jnp.max(most) <= MOST)

    @pl.when(jnp.logical_not(exact))
    def _():
        top[...] = jnp.full_like(top, FLOOR)
        total[...] = jnp.zeros_like(total)

        def step(k, carry):
            index = block(tiles, outer, k, blocks_out)
            found = peaks(k, cost, potential_of(k))
            for h in range(2):
                top[row(index, h), :] = jnp.maximum(top[row(index, h), :], found[h])
            return carry

        lax.fori_loop(0, live, step, 0)
        add_up(2, live, tiles, outer, blocks_out, cost, potential_of, top, total)
        finish(out, top, total)

    if last:
        leave.wait()


def vmem_spec():
    return pl.BlockSpec(memory_space=pltpu.VMEM)


def smem_spec():
    return pl.BlockSpec(memory_space=pltpu.SMEM)


def hbm_spec():
    return pl.BlockSpec(memory_space=pltpu.HBM)


def costs(tiles, counts, src, tgt, blocks_in, blocks_out):
    slots = tiles.shape[1]
    width = src.shape[0]
    part = pltpu.VMEM((slots, 2 * DEPTH, TILE), jnp.bfloat16)
    return pl.pallas_call(
        functools.partial(cost_kernel, blocks_in, blocks_out),
        out_shape=(
            pltpu.VMEM((slots, TILE, TILE), jnp.float32),
            jax.ShapeDtypeStruct((2 * blocks_out, HALF), jnp.float32),
            part,
            part,
            pltpu.SMEM(tiles.shape, jnp.int32),
        ),
        in_specs=[hbm_spec(), smem_spec(), hbm_spec(), hbm_spec()],
        out_specs=(vmem_spec(), vmem_spec(), vmem_spec(), vmem_spec(), smem_spec()),
        scratch_shapes=[
            pltpu.SemaphoreType.DMA(()),
            pltpu.VMEM((slots, width, TILE), jnp.float32),
            pltpu.VMEM((slots, width, TILE), jnp.float32),
            pltpu.VMEM((GROUP, 2, DEPTH, TILE), jnp.float32),
            pltpu.VMEM((2 * blocks_out, HALF), jnp.float32),
            pltpu.VMEM((2 * blocks_out, HALF), jnp.float32),
            pltpu.SemaphoreType.DMA((slots,)),
            pltpu.SemaphoreType.DMA((slots,)),
        ],
        compiler_params=pltpu.CompilerParams(vmem_limit_bytes=VMEM_LIMIT),
    )(tiles, counts, src, tgt)


def turned(counts, lefts, rights):
    slots = lefts.shape[0]
    return pl.pallas_call(
        turn_kernel,
        out_shape=pltpu.VMEM((slots, TILE, TILE), jnp.float32),
        in_specs=[smem_spec(), vmem_spec(), vmem_spec()],
        out_specs=vmem_spec(),
        compiler_params=pltpu.CompilerParams(vmem_limit_bytes=VMEM_LIMIT),
        cost_estimate=pl.CostEstimate(
            flops=slots * 8 * DEPTH * TILE * TILE, bytes_accessed=slots * 8 * TILE * TILE, transcendentals=0
        ),
    )(counts, lefts, rights)


def sweep(tiles, counts, cost, before, parts, cells, far_cells, inner, outer, blocks_in, blocks_out, last):
    far = None if before is None else math.log2(1.0 / far_cells)
    operands = list(parts) if before is None else [before, *parts]
    kernel = functools.partial(
        sweep_kernel, math.log2(1.0 / cells), far, last, inner, outer, blocks_in, blocks_out
    )
    return pl.pallas_call(
        kernel,
        out_shape=(
            jax.ShapeDtypeStruct((2 * blocks_out, HALF), jnp.float32),
            jax.ShapeDtypeStruct((2 * blocks_in, HALF), jnp.float32),
        ),
        in_specs=[smem_spec(), smem_spec()] + [vmem_spec()] * (1 + len(operands)),
        out_specs=(vmem_spec(), hbm_spec() if last else vmem_spec()),
        scratch_shapes=[
            pltpu.VMEM((2, 2 * blocks_in, HALF), jnp.float32),
            pltpu.VMEM((2 * blocks_out, HALF), jnp.float32),
            pltpu.VMEM((2 * blocks_out, HALF), jnp.float32),
            pltpu.SemaphoreType.DMA(()),
        ],
        compiler_params=pltpu.CompilerParams(vmem_limit_bytes=VMEM_LIMIT),
    )(tiles, counts, cost, *operands)


def swap(value, axis, flips):
    src, tgt = lax.axis_size("src"), lax.axis_size("tgt")
    pairs = []
    for s in range(src):
        for t in range(tgt):
            flip = flips[t % 2]
            other = (s ^ flip, t) if axis == "src" else (s, t ^ flip)
            pairs.append((s * tgt + t, other[0] * tgt + other[1]))
    return lax.ppermute(value, ("src", "tgt"), pairs)


def fan(value, axis, *flips):
    return [value, *[swap(value, axis, each) for each in flips]]


def over_core(value):
    return lse2_many(fan(value, "tgt", (1, 1)))


def over_y(value):
    src, tgt = lax.axis_size("src"), lax.axis_size("tgt")
    parts = [value]
    for flip in (2, 4, 6):
        pairs = [(s * tgt + t, s * tgt + (t ^ flip)) for s in range(src) for t in range(1, tgt, 2)]
        parts.append(lax.ppermute(value, ("src", "tgt"), pairs))
    total = lse2_many(parts)
    pairs = [(s * tgt + t, s * tgt + t - 1) for s in range(src) for t in range(1, tgt, 2)]
    other = lax.ppermute(total, ("src", "tgt"), pairs)
    return [jnp.where(lax.axis_index("tgt") % 2 == 1, total, other)]


def over_src(value):
    value = lse2_many(fan(value, "src", (1, 1), (2, 3), (3, 2)))
    for flips in ((4, 4), (12, 28)):
        value = lse2_many(fan(value, "src", flips))
    return fan(value, "src", (28, 12))


def body(src_points, tgt_points, tiles, counts):
    tiles, src_points, tgt_points = (
        pltpu.with_memory_space_constraint(each, pltpu.HBM)
        for each in (tiles[0, 0], src_points, tgt_points)
    )
    row_blocks = src_points.shape[1] // TILE
    col_blocks = tgt_points.shape[1] // TILE
    src_cells = src_points.shape[1] * lax.axis_size("src")
    tgt_cells = tgt_points.shape[1] * lax.axis_size("tgt")
    cost_ba, rows, lefts, rights, tiles = costs(
        tiles, counts, src_points, tgt_points, col_blocks, row_blocks
    )
    target = None
    for turn in range(ITERS):
        last = turn == ITERS - 1
        rows = over_core(rows)
        if turn == 0:
            rows, lefts = lax.optimization_barrier((rows, lefts))
            cost_ab = turned(counts, lefts, rights)
        cols, source = sweep(
            tiles, counts, cost_ab, target, over_y(rows), src_cells, tgt_cells, 0, 1,
            row_blocks, col_blocks, last,
        )
        parts = over_src(cols)
        if last:
            target = (math.log2(1.0 / tgt_cells) - lse2_many(parts)) / SCALE
        else:
            rows, target = sweep(
                tiles, counts, cost_ba, source, parts, tgt_cells, src_cells, 1, 0,
                col_blocks, row_blocks, False,
            )
    return (source.reshape(-1), target.reshape(-1))


def solution(mesh):
    in_specs = (P(None, "src"), P(None, "tgt"), P("src", "tgt", None, None), P("src", "tgt"))
    out_specs = (P("src"), P("tgt"))
    return jax.shard_map(body, mesh=mesh, in_specs=in_specs, out_specs=out_specs, check_vma=False)
```

```python
import functools
import math

import jax
import jax.numpy as jnp
from jax import lax
from jax.experimental import pallas as pl
from jax.experimental.pallas import tpu as pltpu
from jax.sharding import PartitionSpec as P

TILE = 256
HALF = 128
ROWS = 8
GROUP = 8
WIDE = 16
ITERS = 3
EPS = 0.05
FLOOR = -1e30
SCALE = 1.0 / (EPS * math.log(2.0))
DEPTH = 64
LEAST = 2.0**-80
MOST = 2.0**100
VMEM_LIMIT = 16 * 1024 * 1024


def lse2_many(parts):
    top = functools.reduce(jnp.maximum, parts)
    return top + jnp.log2(functools.reduce(jnp.add, [jnp.exp2(p - top) for p in parts]))


def split(value):
    high = value.astype(jnp.bfloat16)
    return high, (value - high.astype(jnp.float32)).astype(jnp.bfloat16)


def halves():
    return [(h, pl.ds(h * HALF, HALF)) for h in range(2)]


def row(index, h):
    return pl.ds(2 * index + h, 1)


def block(tiles, side, k, blocks):
    return jnp.minimum(tiles[side, k], blocks - 1)


def sums(k, cost, potential, shift):
    found = []
    for h, lanes in halves():
        kept = None
        for g, cells in halves():
            score = cost[k, cells, lanes]
            score = (0.0 - score if potential is None else potential[g] - score) - shift[h]
            part = jnp.sum(jnp.exp2(score).reshape(HALF // ROWS, ROWS, HALF), axis=0)
            kept = part if kept is None else kept + part
        found.append(jnp.sum(kept, axis=0, keepdims=True))
    return found


def peaks(k, cost, potential):
    found = []
    for h, lanes in halves():
        kept = None
        for g, cells in halves():
            score = cost[k, cells, lanes]
            score = 0.0 - score if potential is None else potential[g] - score
            part = jnp.max(score, axis=0, keepdims=True)
            kept = part if kept is None else jnp.maximum(kept, part)
        found.append(kept)
    return found


def spread(held, index):
    return [jnp.broadcast_to(held[0, row(index, g), :], (HALF, HALF)).T for g in range(2)]


def add_up(size, live, tiles, outer, blocks_out, cost, potential_of, top, total):
    def group(q, carry):
        least, most = carry
        ready = []
        for u in range(size):
            k = q * size + u
            out = block(tiles, outer, k, blocks_out)
            shift = [top[row(out, h), :] for h in range(2)]
            ready.append((k < live, out, sums(k, cost, potential_of(k), shift)))
        for on, out, found in ready:
            for h in range(2):
                total[row(out, h), :] = total[row(out, h), :] + jnp.where(on, found[h], 0.0)
                least = jnp.minimum(least, jnp.where(on, found[h], 1.0))
                most = jnp.maximum(most, jnp.where(on, found[h], 1.0))
        return least, most

    one = jnp.ones((1, HALF), jnp.float32)
    return lax.fori_loop(0, (live + size - 1) // size, group, (one, one))


def finish(out, top, total):
    found = total[...] > 0.0
    out[...] = jnp.where(found, top[...] + jnp.log2(jnp.where(found, total[...], 1.0)), FLOOR)


def product(first, second):
    turned = first.T
    turned = jnp.concatenate((turned, turned), axis=1)
    high, middle = second[:DEPTH], second[DEPTH:]
    other = jnp.concatenate((high, high, middle, middle), axis=0)
    return jnp.dot(turned, other, preferred_element_type=jnp.float32)


def cost_kernel(
    blocks_in, blocks_out, tiles_in, counts, src, tgt, cost, out, lefts, rights, tiles,
    tsem, xs, ys, ext, top, total, xsem, ysem
):
    table = pltpu.make_async_copy(tiles_in, tiles, tsem)
    table.start()
    width = src.shape[0]
    ext[...] = jnp.zeros_like(ext)
    for u in range(GROUP):
        for side, place in ((0, 1), (0, 3), (1, 0), (1, 2)):
            ext[u, side, pl.ds(width + place, 1), :] = jnp.ones((1, TILE), jnp.float32)
    top[...] = jnp.full_like(top, FLOOR)
    total[...] = jnp.zeros_like(total)
    table.wait()
    live = counts[0, 0]

    def copies(k):
        first = pl.multiple_of(block(tiles, 0, k, blocks_out) * TILE, TILE)
        second = pl.multiple_of(block(tiles, 1, k, blocks_in) * TILE, TILE)
        return (
            pltpu.make_async_copy(src.at[:, pl.ds(first, TILE)], xs.at[k], xsem.at[k]),
            pltpu.make_async_copy(tgt.at[:, pl.ds(second, TILE)], ys.at[k], ysem.at[k]),
        )

    def begin(k, carry):
        for one in copies(k):
            one.start()
        return carry

    def end(k, carry):
        for one in copies(k):
            one.wait()
        return carry

    lax.fori_loop(0, live, begin, 0)

    def extend(u, side, points, scale):
        square = jnp.sum(points * points, axis=0, keepdims=True) * SCALE
        high, middle = split(square)
        ext[u, side, pl.ds(0, width), :] = points * scale
        ext[u, side, pl.ds(width + side, 1), :] = square
        rest = square - high.astype(jnp.float32) - middle.astype(jnp.float32)
        ext[u, side, pl.ds(width + side + 2, 1), :] = rest
        return jnp.concatenate(split(ext[u, side]), axis=0)

    def group(q, carry):
        lax.fori_loop(q * GROUP, jnp.minimum(live, q * GROUP + GROUP), end, 0)
        ready = []
        for u in range(GROUP):
            k = q * GROUP + u
            centre = ys[k, :, pl.ds(0, 1)]
            left = extend(u, 0, xs[k] - centre, -2.0 * SCALE)
            right = extend(u, 1, ys[k] - centre, 1.0)
            lefts[k] = left
            rights[k] = right
            value = product(right, left)
            cost[k] = value
            peak = 0.0 - jnp.min(value, axis=0, keepdims=True)
            ready.append((k < live, block(tiles, 0, k, blocks_out), peak))
        for on, index, peak in ready:
            for h in range(2):
                new = jnp.where(on, peak[:, h * HALF : (h + 1) * HALF], FLOOR)
                top[row(index, h), :] = jnp.maximum(top[row(index, h), :], new)
        return carry

    lax.fori_loop(0, (live + GROUP - 1) // GROUP, group, 0)
    add_up(WIDE, live, tiles, 0, blocks_out, cost, lambda k: None, top, total)
    finish(out, top, total)


def turn_kernel(counts, lefts, rights, cost):
    live = counts[0, 0]

    def group(q, carry):
        for u in range(GROUP):
            k = q * GROUP + u
            cost[k] = product(lefts[k], rights[k])
        return carry

    lax.fori_loop(0, (live + GROUP - 1) // GROUP, group, 0)


def sweep_kernel(offset, far, last, inner, outer, blocks_in, blocks_out, tiles, counts, cost, *refs):
    parts = refs[:-6]
    out, result, held, top, total, rsem = refs[-6:]
    if far is None:
        top[...] = jnp.full_like(top, offset)
    else:
        top[...] = far - parts[0][...]
        parts = parts[1:]
    potential = offset - lse2_many([part[...] for part in parts])
    held[0] = potential
    if last:
        held[1] = potential / SCALE
        leave = pltpu.make_async_copy(held.at[1], result, rsem)
        leave.start()
    else:
        result[...] = potential
    total[...] = jnp.zeros_like(total)
    live = counts[0, 0]

    def potential_of(k):
        return spread(held, block(tiles, inner, k, blocks_in))

    least, most = add_up(WIDE, live, tiles, outer, blocks_out, cost, potential_of, top, total)
    finish(out, top, total)
    exact = (jnp.min(least) >= LEAST) & (jnp.max(most) <= MOST)

    @pl.when(jnp.logical_not(exact))
    def _():
        top[...] = jnp.full_like(top, FLOOR)
        total[...] = jnp.zeros_like(total)

        def step(k, carry):
            index = block(tiles, outer, k, blocks_out)
            found = peaks(k, cost, potential_of(k))
            for h in range(2):
                top[row(index, h), :] = jnp.maximum(top[row(index, h), :], found[h])
            return carry

        lax.fori_loop(0, live, step, 0)
        add_up(2, live, tiles, outer, blocks_out, cost, potential_of, top, total)
        finish(out, top, total)

    if last:
        leave.wait()


def vmem_spec():
    return pl.BlockSpec(memory_space=pltpu.VMEM)


def smem_spec():
    return pl.BlockSpec(memory_space=pltpu.SMEM)


def hbm_spec():
    return pl.BlockSpec(memory_space=pltpu.HBM)


def costs(tiles, counts, src, tgt, blocks_in, blocks_out):
    slots = tiles.shape[1]
    width = src.shape[0]
    part = pltpu.VMEM((slots, 2 * DEPTH, TILE), jnp.bfloat16)
    return pl.pallas_call(
        functools.partial(cost_kernel, blocks_in, blocks_out),
        out_shape=(
            pltpu.VMEM((slots, TILE, TILE), jnp.float32),
            jax.ShapeDtypeStruct((2 * blocks_out, HALF), jnp.float32),
            part,
            part,
            pltpu.SMEM(tiles.shape, jnp.int32),
        ),
        in_specs=[hbm_spec(), smem_spec(), hbm_spec(), hbm_spec()],
        out_specs=(vmem_spec(), vmem_spec(), vmem_spec(), vmem_spec(), smem_spec()),
        scratch_shapes=[
            pltpu.SemaphoreType.DMA(()),
            pltpu.VMEM((slots, width, TILE), jnp.float32),
            pltpu.VMEM((slots, width, TILE), jnp.float32),
            pltpu.VMEM((GROUP, 2, DEPTH, TILE), jnp.float32),
            pltpu.VMEM((2 * blocks_out, HALF), jnp.float32),
            pltpu.VMEM((2 * blocks_out, HALF), jnp.float32),
            pltpu.SemaphoreType.DMA((slots,)),
            pltpu.SemaphoreType.DMA((slots,)),
        ],
        compiler_params=pltpu.CompilerParams(vmem_limit_bytes=VMEM_LIMIT),
    )(tiles, counts, src, tgt)


def turned(counts, lefts, rights):
    slots = lefts.shape[0]
    return pl.pallas_call(
        turn_kernel,
        out_shape=pltpu.VMEM((slots, TILE, TILE), jnp.float32),
        in_specs=[smem_spec(), vmem_spec(), vmem_spec()],
        out_specs=vmem_spec(),
        compiler_params=pltpu.CompilerParams(vmem_limit_bytes=VMEM_LIMIT),
        cost_estimate=pl.CostEstimate(
            flops=slots * 8 * DEPTH * TILE * TILE, bytes_accessed=slots * 8 * TILE * TILE, transcendentals=0
        ),
    )(counts, lefts, rights)


def sweep(tiles, counts, cost, before, parts, cells, far_cells, inner, outer, blocks_in, blocks_out, last):
    far = None if before is None else math.log2(1.0 / far_cells)
    operands = list(parts) if before is None else [before, *parts]
    kernel = functools.partial(
        sweep_kernel, math.log2(1.0 / cells), far, last, inner, outer, blocks_in, blocks_out
    )
    return pl.pallas_call(
        kernel,
        out_shape=(
            jax.ShapeDtypeStruct((2 * blocks_out, HALF), jnp.float32),
            jax.ShapeDtypeStruct((2 * blocks_in, HALF), jnp.float32),
        ),
        in_specs=[smem_spec(), smem_spec()] + [vmem_spec()] * (1 + len(operands)),
        out_specs=(vmem_spec(), hbm_spec() if last else vmem_spec()),
        scratch_shapes=[
            pltpu.VMEM((2, 2 * blocks_in, HALF), jnp.float32),
            pltpu.VMEM((2 * blocks_out, HALF), jnp.float32),
            pltpu.VMEM((2 * blocks_out, HALF), jnp.float32),
            pltpu.SemaphoreType.DMA(()),
        ],
        compiler_params=pltpu.CompilerParams(vmem_limit_bytes=VMEM_LIMIT),
    )(tiles, counts, cost, *operands)


def swap(value, axis, flips):
    src, tgt = lax.axis_size("src"), lax.axis_size("tgt")
    pairs = []
    for s in range(src):
        for t in range(tgt):
            flip = flips[t % 2]
            other = (s ^ flip, t) if axis == "src" else (s, t ^ flip)
            pairs.append((s * tgt + t, other[0] * tgt + other[1]))
    return lax.ppermute(value, ("src", "tgt"), pairs)


def fan(value, axis, *flips):
    return [value, *[swap(value, axis, each) for each in flips]]


def over_core(value):
    return lse2_many(fan(value, "tgt", (1, 1)))


def over_y(value):
    return fan(value, "tgt", (6, 4), (4, 6), (2, 2))


def over_src(value):
    value = lse2_many(fan(value, "src", (3, 3), (2, 2), (1, 1)))
    for flips in ((4, 4), (12, 28)):
        value = lse2_many(fan(value, "src", flips))
    return fan(value, "src", (28, 12))


def body(src_points, tgt_points, tiles, counts):
    tiles, src_points, tgt_points = (
        pltpu.with_memory_space_constraint(each, pltpu.HBM)
        for each in (tiles[0, 0], src_points, tgt_points)
    )
    row_blocks = src_points.shape[1] // TILE
    col_blocks = tgt_points.shape[1] // TILE
    src_cells = src_points.shape[1] * lax.axis_size("src")
    tgt_cells = tgt_points.shape[1] * lax.axis_size("tgt")
    cost_ba, rows, lefts, rights, tiles = costs(
        tiles, counts, src_points, tgt_points, col_blocks, row_blocks
    )
    target = None
    for turn in range(ITERS):
        last = turn == ITERS - 1
        rows = over_core(rows)
        if turn == 0:
            rows, lefts = lax.optimization_barrier((rows, lefts))
            cost_ab = turned(counts, lefts, rights)
        cols, source = sweep(
            tiles, counts, cost_ab, target, over_y(rows), src_cells, tgt_cells, 0, 1,
            row_blocks, col_blocks, last,
        )
        parts = over_src(cols)
        if last:
            target = (math.log2(1.0 / tgt_cells) - lse2_many(parts)) / SCALE
        else:
            rows, target = sweep(
                tiles, counts, cost_ba, source, parts, tgt_cells, src_cells, 1, 0,
                col_blocks, row_blocks, False,
            )
    return (source.reshape(-1), target.reshape(-1))


def solution(mesh):
    in_specs = (P(None, "src"), P(None, "tgt"), P("src", "tgt", None, None), P("src", "tgt"))
    out_specs = (P("src"), P("tgt"))
    return jax.shard_map(body, mesh=mesh, in_specs=in_specs, out_specs=out_specs, check_vma=False)
```
